256 devices in a mesh: dp: 8 (over y, core), expert: 32 (over z, x).
Axes of the slice: x: 4, y: 4, z: 8, core: 2. Of those that a mesh axis runs over, the one named last changes fastest.
Arguments:
- tokens: bfloat16 [8192, 8192], P('expert', 'dp'), may hold values from -6 to 6
- cotangent: bfloat16 [8192, 8192], P('expert', 'dp'), may hold values from -1.5 to 1.5
- route: int32 [8192, 2], P('expert'), may hold values from 0 to 31, all different within a row; in each aligned block of 256 rows (0 to 255, 256 to 511, ...) at most 32 rows name the same one
- score: int32 [8192, 2], P('expert'), may hold values from 1 to 16
- clusters: int32 [14336, 1], P('expert'), may hold values from 0 to 31; in each aligned block of 448 rows (0 to 447, 448 to 895, ...) at most 20 rows name the same one
- w_gate: bfloat16 [14336, 8192], P('expert', 'dp'), may hold values from -0.0625 to 0.0625
- w_up: bfloat16 [14336, 8192], P('expert', 'dp'), may hold values from -0.0625 to 0.0625
- w_down: bfloat16 [14336, 8192], P('expert', 'dp'), may hold values from -0.25 to 0.25
Outputs:
- mixed: bfloat16 [8192, 8192], P('expert', 'dp')
- input_grad: bfloat16 [8192, 8192], P('expert', 'dp')
- grad_gate: bfloat16 [32, 640, 8192], P('expert', None, 'dp')
- grad_up: bfloat16 [32, 640, 8192], P('expert', None, 'dp')
- grad_down: bfloat16 [32, 640, 8192], P('expert', None, 'dp')
The draws below stay inside these ranges and needn't reach their ends.
Inputs may be any that keep to these rules, and one draw needn't show every extreme that they name: `route`: in each aligned block of 256 tokens no expert is named more than 32 times. `clusters`: in each initial shard of 448 consecutive hidden units no expert holds more than 20 of them.
All inputs are finite; a program needn't handle non-finite values.
Results may differ from the reference program's by a relative error of at most 0.029.
Values may be sent and summed in bfloat16 or wider, within the bound.
No kernel may reach another device: no remote copies, remote signals or barrier semaphores. Data moves between devices by JAX's collectives and lax.ppermute only.
A program may use at most 128 MiB of HBM per device.

```python
import math
import jax
import jax.numpy as jnp
import numpy as np
from jax import lax

D = 8192
NEUR_DEV = 448
SLOTS = 640
TOP = 2
TOK_DEV = 256
EXPERTS = 32
FF = 14336
PAIR_CAP = 20
TOK_CAP = 32
TOKENS = 8192
N_DP = 8


def touch_ends(entries, rng, least, top_value):
    longest = entries.shape.index(max(entries.shape))
    spots = []
    for shift in (0, 1):
        where = [jax.random.randint(jax.random.fold_in(rng, axis), (), 0, length) for axis, length in enumerate(entries.shape)]
        where[longest] = (where[longest] + shift) % entries.shape[longest]
        spots.append(tuple(where))
    return entries.at[spots[0]].set(least).at[spots[1]].set(top_value)


def steps_of(key, extent, shards, smallest, high):
    gain, own = 1.0, jax.random.fold_in(key, 6)
    for axis_at, parts in shards:
        steps = jnp.exp(jax.random.uniform(jax.random.fold_in(own, axis_at), (parts,), jnp.float32, smallest / len(shards), high / len(shards)))
        gain = gain * jnp.repeat(steps, extent[axis_at] // parts).reshape([-1 if axis == axis_at else 1 for axis in range(len(extent))])
    return gain


def routed_block(rng, own, number, rows, number_of, top, most, lean):
    order = jax.random.permutation(rng, number_of)
    packed, common = load_shares(number_of, rows * top, most, lean, True), load_shares(number_of, rows * top, most, lean, False)
    places = jnp.arange(number_of)

    def named(tallies, turn):
        used = int((tallies > 0).sum())
        fixed = max(1, used // 4)
        moved = fixed + (places - fixed + turn * (used - fixed)) % max(1, number_of - fixed)
        return jnp.zeros((number_of,), jnp.int32).at[order[jnp.where(places < fixed, places, moved)]].set(jnp.asarray(tallies, jnp.int32))

    tallies = jnp.where(number % 4 == 0, named(packed, number // 4), named(common, number - number // 4 - 1))
    mixed = jax.random.permutation(jax.random.fold_in(own, 3), number_of)
    donor, receiver = mixed[0:number_of // 2 * 2:2], mixed[1:number_of // 2 * 2:2]
    margin = jnp.minimum(tallies[donor] - 1, most - tallies[receiver]) // 2
    margin = jnp.where((donor == order[0]) | (receiver == order[0]) | (tallies[receiver] == 0), 0, jnp.maximum(margin, 0))
    moved = jax.random.randint(jax.random.fold_in(own, 4), (number_of // 2,), 0, 1 << 20) % (margin + 1)
    tallies = tallies.at[donor].add(-moved).at[receiver].add(moved)
    members = jnp.searchsorted(jnp.cumsum(tallies), jnp.arange(rows * top), side="right").astype(jnp.int32)
    grid = members.reshape(top, rows).T
    grid = grid[jax.random.permutation(jax.random.fold_in(own, 1), rows)]
    turn = jax.random.randint(jax.random.fold_in(own, 2), (rows, 1), 0, top)
    return jnp.take_along_axis(grid, (jnp.arange(top)[None, :] + turn) % top, axis=1)


def load_shares(number_of, total, bound, skew, full):
    weights = [(1 << 20) // math.isqrt(rank ** skew) + 1 for rank in range(1, number_of + 1)]
    largest = bound if full else min(bound, max(-(-total // number_of), total * weights[0] // sum(weights)))
    least = 1 if total - largest >= number_of - 1 else 0
    counts, spare = [largest] + [least] * (number_of - 1), total - largest - least * (number_of - 1)
    while spare > 0:
        candidates = [i for i in range(1, number_of) if counts[i] < largest] or [i for i in range(1, number_of) if counts[i] < bound]
        mass, remaining = sum([weights[i] for i in candidates]), spare
        for i in candidates:
            extra = min(bound - counts[i], max(1, remaining * weights[i] // mass), spare)
            counts[i] = counts[i] + extra
            spare = spare - extra
    return np.array(counts)


def normal_values(stream_key, dims, width, limit, pieces=(), kind=jnp.bfloat16):
    gain = steps_of(stream_key, dims, pieces, -0.22, 0.18) if pieces else 1.0
    drawn = jax.random.normal(stream_key, dims, jnp.float32) * width * gain
    return jnp.minimum(jnp.maximum(drawn, -limit), limit).astype(kind)


def setup_inputs(seed: int = 0) -> dict:
    key_of = jax.random.split(jax.random.key(seed), 9)
    tokens = normal_values(key_of[0], (TOKENS, D), 1.0, 6.0, ((0, 32), (1, 8)))
    cotangent = normal_values(key_of[1], (TOKENS, D), 0.25, 1.5, ((0, 32), (1, 8)))
    route_keys = jax.random.split(jax.random.fold_in(key_of[2], 1), TOKENS // TOK_DEV)
    route_turns = jax.random.permutation(jax.random.fold_in(key_of[2], 3), TOKENS // TOK_DEV)
    route = jax.vmap(lambda own, number: routed_block(jax.random.fold_in(key_of[2], 2), own, number, TOK_DEV, EXPERTS, TOP, TOK_CAP, 2))(route_keys, route_turns).reshape((TOKENS, TOP))
    score = touch_ends(jax.random.randint(key_of[3], (TOKENS, TOP), 1, 17), jax.random.fold_in(key_of[3], 1), 1, 16).astype(jnp.int32)
    clusters_keys = jax.random.split(jax.random.fold_in(key_of[4], 1), FF // NEUR_DEV)
    clusters_turns = jax.random.permutation(jax.random.fold_in(key_of[4], 3), FF // NEUR_DEV)
    clusters = jax.vmap(lambda own, number: routed_block(jax.random.fold_in(key_of[4], 2), own, number, NEUR_DEV, EXPERTS, 1, PAIR_CAP, 2))(clusters_keys, clusters_turns).reshape((FF, 1))
    w_gate = normal_values(key_of[5], (FF, D), D ** -0.5, 0.0625, ((0, 32), (1, 8)))
    w_up = normal_values(key_of[6], (FF, D), D ** -0.5, 0.0625, ((0, 32), (1, 8)))
    w_down = normal_values(key_of[7], (FF, D), NEUR_DEV ** -0.5, 0.25, ((0, 32), (1, 8)))
    return {"tokens": tokens, "cotangent": cotangent, "route": route, "score": score, "clusters": clusters, "w_gate": w_gate, "w_up": w_up, "w_down": w_down}


def block_rank(ids, count, blocks):
    onehot = (ids[:, None] == jnp.arange(count, dtype=jnp.int32)[None, :]).astype(jnp.int32)
    grouped = onehot.reshape(blocks, -1, count)
    before = (jnp.cumsum(grouped, axis=1) - grouped).reshape(-1, count)
    return jnp.sum(before * onehot, axis=1).astype(jnp.int32)


def sliced_product(left, right):
    left3 = left.astype(jnp.float32).reshape(left.shape[0], N_DP, -1)
    right3 = right.astype(jnp.float32).reshape(right.shape[0], N_DP, -1)
    partial_value = jnp.einsum('rnd,snd->nrs', left3, right3, precision=lax.Precision.HIGHEST)
    rounded = lax.optimization_barrier(partial_value.astype(jnp.bfloat16))
    return jnp.sum(rounded.astype(jnp.float32), axis=0)


def one_expert(inputs):
    rows_x, rows_dy, gate_w, up_w, down_w = inputs
    gate = sliced_product(rows_x, gate_w)
    upper = sliced_product(rows_x, up_w)
    sig = jax.nn.sigmoid(gate)
    act = gate * sig
    hidden = (act * upper).astype(jnp.bfloat16)
    out_rows = jnp.dot(hidden, down_w, preferred_element_type=jnp.float32).astype(jnp.bfloat16)
    back = sliced_product(rows_dy, down_w)
    d_gate = (back * upper * sig * (1.0 + gate * (1.0 - sig))).astype(jnp.bfloat16)
    d_up = (back * act).astype(jnp.bfloat16)
    grad_down = jnp.dot(hidden.T, rows_dy, preferred_element_type=jnp.float32).astype(jnp.bfloat16)
    grad_gate = jnp.dot(d_gate.T, rows_x, preferred_element_type=jnp.float32).astype(jnp.bfloat16)
    grad_up = jnp.dot(d_up.T, rows_x, preferred_element_type=jnp.float32).astype(jnp.bfloat16)
    in_rows = (jnp.dot(d_gate, gate_w, preferred_element_type=jnp.float32)
               + jnp.dot(d_up, up_w, preferred_element_type=jnp.float32)).astype(jnp.bfloat16)
    return out_rows, in_rows, grad_gate, grad_up, grad_down


def reference(tokens, cotangent, route, score, clusters, w_gate, w_up, w_down):
    pair_cap = SLOTS // EXPERTS
    neuron_ids = clusters[:, 0].astype(jnp.int32)
    source = jnp.arange(FF, dtype=jnp.int32) // NEUR_DEV
    place = neuron_ids * SLOTS + source * pair_cap + block_rank(neuron_ids, EXPERTS, FF // NEUR_DEV)

    def relay(weight):
        return jnp.zeros((EXPERTS * SLOTS, D), weight.dtype).at[place].set(weight).reshape(EXPERTS, SLOTS, D)

    gate_rows, up_rows, down_rows = relay(w_gate), relay(w_up), relay(w_down)
    rows_each = EXPERTS * TOK_CAP
    chosen = route.reshape(-1).astype(jnp.int32)
    block_of = jnp.arange(TOKENS * TOP, dtype=jnp.int32) // (TOK_DEV * TOP)
    position = chosen * rows_each + block_of * TOK_CAP + block_rank(chosen, EXPERTS, TOKENS // TOK_DEV)
    shares = score.astype(jnp.float32)
    shares = (shares / jnp.sum(shares, axis=1, keepdims=True)).reshape(-1)
    repeated = jnp.repeat(tokens, TOP, axis=0)
    scaled = (shares[:, None] * jnp.repeat(cotangent, TOP, axis=0).astype(jnp.float32)).astype(jnp.bfloat16)
    expert_tokens = jnp.zeros((EXPERTS * rows_each, D), jnp.bfloat16).at[position].set(repeated)
    expert_grads = jnp.zeros((EXPERTS * rows_each, D), jnp.bfloat16).at[position].set(scaled)
    results = lax.map(one_expert, (expert_tokens.reshape(EXPERTS, rows_each, D),
                                   expert_grads.reshape(EXPERTS, rows_each, D),
                                   gate_rows, up_rows, down_rows))
    out_rows, in_rows, grad_gate, grad_up, grad_down = results
    picked_out = out_rows.reshape(-1, D)[position].astype(jnp.float32)
    picked_in = in_rows.reshape(-1, D)[position].astype(jnp.float32)
    mixed = jnp.sum((shares[:, None] * picked_out).reshape(TOKENS, TOP, D), axis=1).astype(jnp.bfloat16)
    input_grad = jnp.sum(picked_in.reshape(TOKENS, TOP, D), axis=1).astype(jnp.bfloat16)
    return mixed, input_grad, grad_gate, grad_up, grad_down
```

```python
import functools

import jax
import jax.numpy as jnp
from jax import lax
from jax.experimental import pallas as pl
from jax.experimental.pallas import tpu as pltpu
from jax.sharding import Mesh
from jax.sharding import PartitionSpec as P

SLOTS = 640
EXPERT = ("z", "x")
DP = ("y", "core")
BF16 = jnp.bfloat16
F32 = jnp.float32
LIMIT = 48 * 1024 * 1024


def iota(shape, axis):
    return lax.broadcasted_iota(jnp.int32, shape, axis)


def kernel_call(body, name, **kwargs):
    return pl.pallas_call(
        body,
        name=name,
        compiler_params=pltpu.CompilerParams(vmem_limit_bytes=LIMIT),
        **kwargs,
    )


def ranks(rows, count):
    n = rows[0].shape[1]
    hits = [iota((count, n), 0) == ids for ids in rows]
    seen = sum(hit.astype(F32) for hit in hits).astype(BF16)
    earlier = (iota((n, n), 0) < iota((n, n), 1)).astype(F32).astype(BF16)
    before = jnp.dot(seen, earlier, preferred_element_type=F32)
    return [
        jnp.sum(jnp.where(hit, before, 0.0), axis=0, keepdims=True).astype(jnp.int32)
        for hit in hits
    ]


def token_places(route_ref, experts, cap):
    rows = [route_ref[0:1, :], route_ref[1:2, :]]
    return [ids * cap + rank for ids, rank in zip(rows, ranks(rows, experts))]


def token_shares(score_ref):
    score = score_ref[...].astype(F32)
    first, second = score[0:1, :], score[1:2, :]
    total = first + second
    return first / total, second / total


def dispatch_body(scaled, experts, cap, route_ref, score_ref, x_ref, out_ref):
    block, count = out_ref.shape[0], x_ref.shape[0]
    places = token_places(route_ref, experts, cap)
    slot = iota((block, count), 0) + pl.program_id(0) * block
    hits = [slot == place for place in places]
    pick = jnp.where(hits[0] | hits[1], 1.0, 0.0).astype(BF16)
    rows = jnp.dot(pick, x_ref[...], preferred_element_type=F32)
    if scaled:
        shares = token_shares(score_ref)
        weight = jnp.where(hits[0], shares[0], 0.0) + jnp.where(hits[1], shares[1], 0.0)
        rows = rows * jnp.sum(weight, axis=1, keepdims=True)
    out_ref[...] = rows.astype(BF16)


def dispatch(route, score, x, experts, cap, scaled):
    count, width = x.shape
    block = 256
    total = experts * cap
    whole = lambda i: (0, 0)
    return kernel_call(
        functools.partial(dispatch_body, scaled, experts, cap),
        "dispatch",
        grid=(total // block,),
        in_specs=[
            pl.BlockSpec((2, count), whole),
            pl.BlockSpec((2, count), whole),
            pl.BlockSpec((count, width), whole),
        ],
        out_specs=pl.BlockSpec((block, width), lambda i: (i, 0)),
        out_shape=jax.ShapeDtypeStruct((total, width), BF16),
    )(route, score, x)


def pack_body(experts, cap, ids_ref, a_ref, b_ref, out_ref):
    block, count = out_ref.shape[0], a_ref.shape[0]
    ids = ids_ref[...]
    place = ids * (2 * cap) + ranks([ids], experts)[0]
    slot = iota((block, count), 0) + pl.program_id(0) * block
    pick_a = jnp.where(slot == place, 1.0, 0.0).astype(BF16)
    pick_b = jnp.where(slot == place + cap, 1.0, 0.0).astype(BF16)
    out_ref[...] = (
        jnp.dot(pick_a, a_ref[...], preferred_element_type=F32)
        + jnp.dot(pick_b, b_ref[...], preferred_element_type=F32)
    ).astype(BF16)


def pack(ids, a, b, experts, cap, width, columns):
    count = a.shape[0]
    block = 256
    total = 2 * experts * cap
    whole = lambda i: (0, 0)
    return kernel_call(
        functools.partial(pack_body, experts, cap),
        "pack",
        grid=(total // block,),
        in_specs=[
            pl.BlockSpec((1, count), whole),
            pl.BlockSpec((count, width), lambda i: (0, columns[0])),
            pl.BlockSpec((count, width), lambda i: (0, columns[1])),
        ],
        out_specs=pl.BlockSpec((block, width), lambda i: (i, 0)),
        out_shape=jax.ShapeDtypeStruct((total, width), BF16),
    )(ids, a, b)


def unpack_picks(block, cap):
    row, column = iota((block, 2 * block), 0), iota((block, 2 * block), 1)
    group = sum((row >= g * cap).astype(jnp.int32) for g in range(1, block // cap))
    first = row + cap * group
    return [jnp.where(column == first + k * cap, 1.0, 0.0).astype(BF16) for k in (0, 1)]


def unpack_two_body(cap, raw_ref, out_ref):
    picks = unpack_picks(out_ref.shape[1], cap)
    raw = raw_ref[...]
    for k in (0, 1):
        out_ref[k] = jnp.dot(picks[k], raw, preferred_element_type=F32).astype(BF16)


def unpack_one_body(cap, raw_ref, out_ref):
    width = raw_ref.shape[1]
    picks = unpack_picks(out_ref.shape[0], cap)
    raw = raw_ref[...]
    for k in (0, 1):
        out_ref[:, k * width : (k + 1) * width] = jnp.dot(
            picks[k], raw, preferred_element_type=F32
        ).astype(BF16)


def unpack_two(raw, cap):
    rows, width = raw.shape[0] // 2, raw.shape[1]
    block = 160
    return kernel_call(
        functools.partial(unpack_two_body, cap),
        "unpack_two",
        grid=(rows // block,),
        in_specs=[pl.BlockSpec((2 * block, width), lambda i: (i, 0))],
        out_specs=pl.BlockSpec((2, block, width), lambda i: (0, i, 0)),
        out_shape=jax.ShapeDtypeStruct((2, rows, width), BF16),
    )(raw).reshape(2 * rows, width)


def unpack_one(raw, cap):
    rows, width = raw.shape[0] // 2, raw.shape[1]
    block = 160
    return kernel_call(
        functools.partial(unpack_one_body, cap),
        "unpack_one",
        grid=(rows // block,),
        in_specs=[pl.BlockSpec((2 * block, width), lambda i: (i, 0))],
        out_specs=pl.BlockSpec((block, 2 * width), lambda i: (i, 0)),
        out_shape=jax.ShapeDtypeStruct((rows, 2 * width), BF16),
    )(raw)


def column_of(row):
    n = row.shape[1]
    same = iota((n, n), 0) == iota((n, n), 1)
    return jnp.sum(jnp.where(same, row, jnp.zeros_like(row)), axis=1, keepdims=True)


def combine_body(scaled, experts, cap, route_ref, score_ref, rows_ref, out_ref):
    count, total = out_ref.shape[0], rows_ref.shape[0]
    places = [column_of(place) for place in token_places(route_ref, experts, cap)]
    slot = iota((count, total), 1)
    hits = [slot == place for place in places]
    rows = rows_ref[...]
    if scaled:
        shares = [column_of(share) for share in token_shares(score_ref)]
        weight = jnp.where(hits[0], shares[0], 0.0) + jnp.where(hits[1], shares[1], 0.0)
        high = weight.astype(BF16)
        low = (weight - high.astype(F32)).astype(BF16)
        total_rows = jnp.dot(high, rows, preferred_element_type=F32) + jnp.dot(
            low, rows, preferred_element_type=F32
        )
    else:
        pick = jnp.where(hits[0] | hits[1], 1.0, 0.0).astype(BF16)
        total_rows = jnp.dot(pick, rows, preferred_element_type=F32)
    out_ref[...] = total_rows.astype(BF16)


def combine(route, score, rows, experts, cap, scaled):
    count = route.shape[1]
    total, width = rows.shape
    block = 512
    whole = lambda i: (0, 0)
    return kernel_call(
        functools.partial(combine_body, scaled, experts, cap),
        "combine",
        grid=(width // block,),
        in_specs=[
            pl.BlockSpec((2, count), whole),
            pl.BlockSpec((2, count), whole),
            pl.BlockSpec((total, block), lambda i: (0, i)),
        ],
        out_specs=pl.BlockSpec((count, block), lambda i: (0, i)),
        out_shape=jax.ShapeDtypeStruct((count, width), BF16),
    )(route, score, rows)


def exchange(rows, parts):
    total, width = rows.shape
    return lax.all_to_all(
        rows.reshape(parts, total // parts, width),
        EXPERT,
        split_axis=0,
        concat_axis=0,
        tiled=True,
    ).reshape(total, width)


def after(value, other):
    return lax.optimization_barrier((value, other))[0]


def shift(value, axis, step):
    size = lax.axis_size(axis)
    return lax.ppermute(value, axis, [(i, (i + step) % size) for i in range(size)])


def pick(value, index, axis):
    return lax.dynamic_index_in_dim(value, index, axis, keepdims=False)


def put(value, part, y, core):
    return lax.dynamic_update_slice(value, part[None, None], (y, core, 0, 0))


def scatter_sum(value):
    rows, n = value.shape
    ys, cores = lax.axis_size("y"), lax.axis_size("core")
    y, core = lax.axis_index("y"), lax.axis_index("core")
    value = value.reshape(ys, cores, rows // (ys * cores), n)
    other = shift(pick(value, 1 - core, 1), "core", 1)
    pair = (pick(value, core, 1).astype(F32) + other.astype(F32)).astype(BF16)
    half = n // 2
    far = pick(pair, (y + 2) % ys, 0)
    low = shift(far[:, :half], "y", 1).astype(F32)
    high = shift(far[:, half:], "y", -1).astype(F32)
    above = pick(pair, (y + 1) % ys, 0).astype(F32)
    below = pick(pair, (y + ys - 1) % ys, 0).astype(F32)
    to_above = jnp.concatenate([above[:, :half] + low, above[:, half:]], axis=1)
    to_below = jnp.concatenate([below[:, :half], below[:, half:] + high], axis=1)
    from_below = shift(to_above.astype(BF16), "y", 1).astype(F32)
    from_above = shift(to_below.astype(BF16), "y", -1).astype(F32)
    return pick(pair, y, 0).astype(F32) + from_below + from_above


def gather_blocks(part):
    rows, n = part.shape
    ys, cores = lax.axis_size("y"), lax.axis_size("core")
    y, core = lax.axis_index("y"), lax.axis_index("core")
    half = n // 2
    from_below = shift(part, "y", 1)
    from_above = shift(part, "y", -1)
    low = shift(from_below[:, :half], "y", 1)
    high = shift(from_above[:, half:], "y", -1)
    far = jnp.concatenate([low, high], axis=1)
    column = jnp.zeros((ys, rows, n), part.dtype)
    for k, piece in enumerate((part, from_below, far, from_above)):
        column = lax.dynamic_update_slice(column, piece[None], ((y + ys - k) % ys, 0, 0))
    other = shift(column, "core", 1)
    both = jnp.where(
        core == 0, jnp.stack([column, other], axis=1), jnp.stack([other, column], axis=1)
    )
    return both.reshape(ys * cores * rows, n)


def activate(gate, upper):
    sig = jax.nn.sigmoid(gate)
    return (gate * sig * upper).astype(BF16)


def backprop(back, gate, upper):
    sig = jax.nn.sigmoid(gate)
    d_gate = (back * upper * sig * (1.0 + gate * (1.0 - sig))).astype(BF16)
    d_up = (back * gate * sig).astype(BF16)
    return jnp.concatenate([d_gate, d_up], axis=1)


def body(tokens, cotangent, route, score, clusters, w_gate, w_up, w_down):
    experts = lax.axis_size(EXPERT)
    pair_cap = SLOTS // experts
    tok_count, width = tokens.shape
    tok_cap = 4 * tok_count // experts
    route, score, ids = route.T, score.T, clusters.T
    contract = (((1,), (1,)), ((), ()))
    over_rows = (((0,), (0,)), ((), ()))

    sent_tokens = dispatch(route, score, tokens, experts, tok_cap, False)
    rows_x = exchange(sent_tokens, experts)
    packed = pack(ids, w_gate, w_up, experts, pair_cap, width, (0, 0))
    raw = exchange(after(packed, rows_x), experts)
    packed_down = pack(ids, w_down, w_down, experts, pair_cap, width // 2, (0, 1))
    raw_down = exchange(after(packed_down, raw), experts)

    gate_up_rows = unpack_two(raw, pair_cap)
    part = lax.dot_general(rows_x, gate_up_rows, contract, preferred_element_type=F32)
    part = part.astype(BF16)
    sent_grads = dispatch(route, score, cotangent, experts, tok_cap, True)
    rows_dy = exchange(after(sent_grads, (raw_down, part)), experts)
    gate_up = scatter_sum(part)
    gate, upper = gate_up[:, :SLOTS], gate_up[:, SLOTS:]
    hidden = gather_blocks(activate(gate, upper))
    down_rows = unpack_one(raw_down, pair_cap)
    out_part = jnp.dot(hidden, down_rows, preferred_element_type=F32).astype(BF16)
    out_part, rows_dy = lax.optimization_barrier((out_part, rows_dy))
    back_out = exchange(out_part, experts)

    back_part = lax.dot_general(rows_dy, down_rows, contract, preferred_element_type=F32)
    back = scatter_sum(back_part.astype(BF16))
    d_both = gather_blocks(backprop(back, gate, upper))
    input_part = jnp.dot(d_both, gate_up_rows, preferred_element_type=F32).astype(BF16)
    back_in = exchange(after(input_part, back_out), experts)

    d_both, hidden, rows_dy = after((d_both, hidden, rows_dy), input_part)
    grad_down = lax.dot_general(hidden, rows_dy, over_rows, preferred_element_type=F32)
    grad_gate = lax.dot_general(
        d_both[:, :SLOTS], rows_x, over_rows, preferred_element_type=F32
    )
    grad_up = lax.dot_general(d_both[:, SLOTS:], rows_x, over_rows, preferred_element_type=F32)
    mixed = combine(route, score, back_out, experts, tok_cap, True)
    input_grad = combine(route, score, back_in, experts, tok_cap, False)
    return (
        mixed,
        input_grad,
        grad_gate.astype(BF16)[None],
        grad_up.astype(BF16)[None],
        grad_down.astype(BF16)[None],
    )


def solution(mesh):
    fine = Mesh(mesh.devices.reshape(4, 2, 8, 4), DP + EXPERT)
    full, rows_only = P(EXPERT, DP), P(EXPERT, None)
    grads = P(EXPERT, None, DP)
    return jax.shard_map(
        body,
        mesh=fine,
        in_specs=(full, full, rows_only, rows_only, rows_only, full, full, full),
        out_specs=(full, full, grads, grads, grads),
        check_vma=False,
    )
```

```python
import functools

import jax
import jax.numpy as jnp
from jax import lax
from jax.experimental import pallas as pl
from jax.experimental.pallas import tpu as pltpu
from jax.sharding import Mesh
from jax.sharding import PartitionSpec as P

SLOTS = 640
EXPERT = ("z", "x")
DP = ("y", "core")
BF16 = jnp.bfloat16
F32 = jnp.float32
LIMIT = 48 * 1024 * 1024


def iota(shape, axis):
    return lax.broadcasted_iota(jnp.int32, shape, axis)


def kernel_call(body, name, **kwargs):
    return pl.pallas_call(
        body,
        name=name,
        compiler_params=pltpu.CompilerParams(vmem_limit_bytes=LIMIT),
        **kwargs,
    )


def ranks(rows, count):
    n = rows[0].shape[1]
    hits = [iota((count, n), 0) == ids for ids in rows]
    seen = sum(hit.astype(F32) for hit in hits).astype(BF16)
    earlier = (iota((n, n), 0) < iota((n, n), 1)).astype(F32).astype(BF16)
    before = jnp.dot(seen, earlier, preferred_element_type=F32)
    return [
        jnp.sum(jnp.where(hit, before, 0.0), axis=0, keepdims=True).astype(jnp.int32)
        for hit in hits
    ]


def token_places(route_ref, experts, cap):
    rows = [route_ref[0:1, :], route_ref[1:2, :]]
    return [ids * cap + rank for ids, rank in zip(rows, ranks(rows, experts))]


def token_shares(score_ref):
    score = score_ref[...].astype(F32)
    first, second = score[0:1, :], score[1:2, :]
    total = first + second
    return first / total, second / total


def dispatch_body(scaled, experts, cap, *refs):
    route_ref, x_ref, out_ref = refs[0], refs[-2], refs[-1]
    block, count = out_ref.shape[0], x_ref.shape[0]
    places = token_places(route_ref, experts, cap)
    slot = iota((block, count), 0) + pl.program_id(0) * block
    hits = [slot == place for place in places]
    pick = jnp.where(hits[0] | hits[1], 1.0, 0.0).astype(BF16)
    rows = jnp.dot(pick, x_ref[...], preferred_element_type=F32)
    if scaled:
        shares = token_shares(refs[1])
        weight = jnp.where(hits[0], shares[0], 0.0) + jnp.where(hits[1], shares[1], 0.0)
        rows = rows * jnp.sum(weight, axis=1, keepdims=True)
    out_ref[...] = rows.astype(BF16)


def dispatch(route, score, x, experts, cap, scaled):
    count, width = x.shape
    block = 256
    total = experts * cap
    whole = lambda i: (0, 0)
    return kernel_call(
        functools.partial(dispatch_body, scaled, experts, cap),
        "dispatch",
        grid=(total // block,),
        in_specs=[pl.BlockSpec((2, count), whole)] * (2 if scaled else 1)
        + [pl.BlockSpec((count, width), whole)],
        out_specs=pl.BlockSpec((block, width), lambda i: (i, 0)),
        out_shape=jax.ShapeDtypeStruct((total, width), BF16),
    )(*((route, score) if scaled else (route,)), x)


def pack_body(experts, cap, ids_ref, a_ref, b_ref, out_ref):
    block, count = out_ref.shape[0], a_ref.shape[0]
    ids = ids_ref[...]
    place = ids * (2 * cap) + ranks([ids], experts)[0]
    slot = iota((block, count), 0) + pl.program_id(0) * block
    pick_a = jnp.where(slot == place, 1.0, 0.0).astype(BF16)
    pick_b = jnp.where(slot == place + cap, 1.0, 0.0).astype(BF16)
    out_ref[...] = (
        jnp.dot(pick_a, a_ref[...], preferred_element_type=F32)
        + jnp.dot(pick_b, b_ref[...], preferred_element_type=F32)
    ).astype(BF16)


def pack(ids, a, b, experts, cap, width, columns):
    count = a.shape[0]
    block = 256
    total = 2 * experts * cap
    whole = lambda i: (0, 0)
    return kernel_call(
        functools.partial(pack_body, experts, cap),
        "pack",
        grid=(total // block,),
        in_specs=[
            pl.BlockSpec((1, count), whole),
            pl.BlockSpec((count, width), lambda i: (0, columns[0])),
            pl.BlockSpec((count, width), lambda i: (0, columns[1])),
        ],
        out_specs=pl.BlockSpec((block, width), lambda i: (i, 0)),
        out_shape=jax.ShapeDtypeStruct((total, width), BF16),
    )(ids, a, b)


def unpack_picks(block, cap):
    row, column = iota((block, 2 * block), 0), iota((block, 2 * block), 1)
    group = sum((row >= g * cap).astype(jnp.int32) for g in range(1, block // cap))
    first = row + cap * group
    return [jnp.where(column == first + k * cap, 1.0, 0.0).astype(BF16) for k in (0, 1)]


def unpack_two_body(cap, raw_ref, out_ref):
    picks = unpack_picks(out_ref.shape[1], cap)
    raw = raw_ref[...]
    for k in (0, 1):
        out_ref[k] = jnp.dot(picks[k], raw, preferred_element_type=F32).astype(BF16)


def unpack_one_body(cap, raw_ref, out_ref):
    width = raw_ref.shape[1]
    picks = unpack_picks(out_ref.shape[0], cap)
    raw = raw_ref[...]
    for k in (0, 1):
        out_ref[:, k * width : (k + 1) * width] = jnp.dot(
            picks[k], raw, preferred_element_type=F32
        ).astype(BF16)


def unpack_two(raw, cap):
    rows, width = raw.shape[0] // 2, raw.shape[1]
    block = 160
    return kernel_call(
        functools.partial(unpack_two_body, cap),
        "unpack_two",
        grid=(rows // block,),
        in_specs=[pl.BlockSpec((2 * block, width), lambda i: (i, 0))],
        out_specs=pl.BlockSpec((2, block, width), lambda i: (0, i, 0)),
        out_shape=jax.ShapeDtypeStruct((2, rows, width), BF16),
    )(raw).reshape(2 * rows, width)


def unpack_one(raw, cap):
    rows, width = raw.shape[0] // 2, raw.shape[1]
    block = 160
    return kernel_call(
        functools.partial(unpack_one_body, cap),
        "unpack_one",
        grid=(rows // block,),
        in_specs=[pl.BlockSpec((2 * block, width), lambda i: (i, 0))],
        out_specs=pl.BlockSpec((block, 2 * width), lambda i: (i, 0)),
        out_shape=jax.ShapeDtypeStruct((rows, 2 * width), BF16),
    )(raw)


FREE = pl.CostEstimate(flops=0, bytes_accessed=0, transcendentals=0)


def add_half_body(start, rows_ref, half_ref, out_ref):
    width = half_ref.shape[1]
    out_ref[...] = rows_ref[...]
    side = (slice(None), slice(start, start + width))
    out_ref[side] = (rows_ref[side].astype(F32) + half_ref[...].astype(F32)).astype(BF16)


def add_half(rows, half, start):
    return kernel_call(
        functools.partial(add_half_body, start),
        "add_half",
        out_shape=jax.ShapeDtypeStruct(rows.shape, BF16),
        cost_estimate=FREE,
    )(rows, half)


def sum_three(refs):
    return sum(ref[...].astype(F32) for ref in refs)


def hidden_body(own_ref, below_ref, above_ref, hidden_ref, sums_ref):
    sums = sum_three((own_ref, below_ref, above_ref))
    sums_ref[...] = sums
    hidden_ref[...] = activate(sums[:, :SLOTS], sums[:, SLOTS:])


def hidden_of(parts):
    rows, n = parts[0].shape
    return kernel_call(
        hidden_body,
        "hidden",
        out_shape=[
            jax.ShapeDtypeStruct((rows, n // 2), BF16),
            jax.ShapeDtypeStruct((rows, n), F32),
        ],
        cost_estimate=FREE,
    )(*parts)


def backprop_body(own_ref, below_ref, above_ref, sums_ref, out_ref):
    back = sum_three((own_ref, below_ref, above_ref))
    d_gate, d_up = backprop(back, sums_ref[:, :SLOTS], sums_ref[:, SLOTS:])
    out_ref[:, :SLOTS] = d_gate
    out_ref[:, SLOTS:] = d_up


def backprop_of(parts, sums):
    return kernel_call(
        backprop_body,
        "backprop",
        out_shape=jax.ShapeDtypeStruct(sums.shape, BF16),
        cost_estimate=FREE,
    )(*parts, sums)


def interleave_body(core_ref, own_ref, other_ref, out_ref):
    core = core_ref[0]
    out_ref[:, core] = own_ref[...]
    out_ref[:, 1 - core] = other_ref[...]


def interleave(own, other, core):
    ys, rows, n = own.shape
    return kernel_call(
        interleave_body,
        "interleave",
        in_specs=[
            pl.BlockSpec(memory_space=pltpu.SMEM),
            pl.BlockSpec(memory_space=pltpu.VMEM),
            pl.BlockSpec(memory_space=pltpu.VMEM),
        ],
        out_shape=jax.ShapeDtypeStruct((ys, 2, rows, n), own.dtype),
        cost_estimate=FREE,
    )(core[None], own, other)


def product_body(dims, a_ref, b_ref, out_ref):
    out_ref[...] = lax.dot_general(
        a_ref[...], b_ref[...], dims, preferred_element_type=F32
    ).astype(BF16)


def product(a, b, transposed):
    rows, depth = a.shape
    n = b.shape[0 if transposed else 1]
    block = 256
    dims = (((1,), (1 if transposed else 0,)), ((), ()))
    return kernel_call(
        functools.partial(product_body, dims),
        "product",
        grid=(rows // block,),
        in_specs=[
            pl.BlockSpec((block, depth), lambda i: (i, 0)),
            pl.BlockSpec(b.shape, lambda i: (0, 0)),
        ],
        out_specs=pl.BlockSpec((block, n), lambda i: (i, 0)),
        out_shape=jax.ShapeDtypeStruct((rows, n), BF16),
        cost_estimate=FREE,
    )(a, b)


def column_of(row):
    n = row.shape[1]
    same = iota((n, n), 0) == iota((n, n), 1)
    return jnp.sum(jnp.where(same, row, jnp.zeros_like(row)), axis=1, keepdims=True)


def combine_body(scaled, experts, cap, *refs):
    route_ref, rows_ref, out_ref = refs[0], refs[-2], refs[-1]
    count, total = out_ref.shape[0], rows_ref.shape[0]
    places = [column_of(place) for place in token_places(route_ref, experts, cap)]
    slot = iota((count, total), 1)
    hits = [slot == place for place in places]
    rows = rows_ref[...]
    if scaled:
        shares = [column_of(share) for share in token_shares(refs[1])]
        weight = jnp.where(hits[0], shares[0], 0.0) + jnp.where(hits[1], shares[1], 0.0)
        high = weight.astype(BF16)
        low = (weight - high.astype(F32)).astype(BF16)
        total_rows = jnp.dot(high, rows, preferred_element_type=F32) + jnp.dot(
            low, rows, preferred_element_type=F32
        )
    else:
        pick = jnp.where(hits[0] | hits[1], 1.0, 0.0).astype(BF16)
        total_rows = jnp.dot(pick, rows, preferred_element_type=F32)
    out_ref[...] = total_rows.astype(BF16)


def combine(route, score, rows, experts, cap, scaled):
    count = route.shape[1]
    total, width = rows.shape
    block = 512
    whole = lambda i: (0, 0)
    return kernel_call(
        functools.partial(combine_body, scaled, experts, cap),
        "combine",
        grid=(width // block,),
        in_specs=[pl.BlockSpec((2, count), whole)] * (2 if scaled else 1)
        + [pl.BlockSpec((total, block), lambda i: (0, i))],
        out_specs=pl.BlockSpec((count, block), lambda i: (0, i)),
        out_shape=jax.ShapeDtypeStruct((count, width), BF16),
    )(*((route, score) if scaled else (route,)), rows)


def exchange(rows, parts):
    total, width = rows.shape
    return lax.all_to_all(
        rows.reshape(parts, total // parts, width),
        EXPERT,
        split_axis=0,
        concat_axis=0,
        tiled=True,
    ).reshape(total, width)


def after(value, other):
    return lax.optimization_barrier((value, other))[0]


def shift(value, axis, step):
    size = lax.axis_size(axis)
    return lax.ppermute(value, axis, [(i, (i + step) % size) for i in range(size)])


def pick(value, index, axis):
    return lax.dynamic_index_in_dim(value, index, axis, keepdims=False)


def put(value, part, y, core):
    return lax.dynamic_update_slice(value, part[None, None], (y, core, 0, 0))


def scatter_sum(value):
    rows, n = value.shape
    ys, cores = lax.axis_size("y"), lax.axis_size("core")
    y, core = lax.axis_index("y"), lax.axis_index("core")
    value = value.reshape(ys, cores, rows // (ys * cores), n)
    other = shift(pick(value, 1 - core, 1), "core", 1)
    pair = (pick(value, core, 1).astype(F32) + other.astype(F32)).astype(BF16)
    half = n // 256 * 128
    far = pick(pair, (y + 2) % ys, 0)
    low = shift(far[:, :half], "y", 1)
    high = shift(far[:, half:], "y", -1)
    to_above = add_half(pick(pair, (y + 1) % ys, 0), low, 0)
    to_below = add_half(pick(pair, (y + ys - 1) % ys, 0), high, half)
    return pick(pair, y, 0), shift(to_above, "y", 1), shift(to_below, "y", -1)


def gather_blocks(part):
    rows, n = part.shape
    ys, cores = lax.axis_size("y"), lax.axis_size("core")
    y, core = lax.axis_index("y"), lax.axis_index("core")
    half = n // 256 * 128
    from_below = shift(part, "y", 1)
    from_above = shift(part, "y", -1)
    low = shift(from_below[:, :half], "y", 1)
    high = shift(from_above[:, half:], "y", -1)
    far = jnp.concatenate([low, high], axis=1)
    column = jnp.zeros((ys, rows, n), part.dtype)
    for k, piece in enumerate((part, from_below, far, from_above)):
        column = lax.dynamic_update_slice(column, piece[None], ((y + ys - k) % ys, 0, 0))
    other = shift(column, "core", 1)
    return interleave(column, other, core).reshape(ys * cores * rows, n)


def activate(gate, upper):
    sig = jax.nn.sigmoid(gate)
    return (gate * sig * upper).astype(BF16)


def backprop(back, gate, upper):
    sig = jax.nn.sigmoid(gate)
    d_gate = (back * upper * sig * (1.0 + gate * (1.0 - sig))).astype(BF16)
    d_up = (back * gate * sig).astype(BF16)
    return d_gate, d_up


def body(tokens, cotangent, route, score, clusters, w_gate, w_up, w_down):
    experts = lax.axis_size(EXPERT)
    pair_cap = SLOTS // experts
    tok_count, width = tokens.shape
    tok_cap = 4 * tok_count // experts
    route, score, ids = route.T, score.T, clusters.T
    over_rows = (((0,), (0,)), ((), ()))

    sent_tokens = dispatch(route, score, tokens, experts, tok_cap, False)
    rows_x = exchange(sent_tokens, experts)
    packed = pack(ids, w_gate, w_up, experts, pair_cap, width, (0, 0))
    raw = exchange(after(packed, rows_x), experts)
    packed_down = pack(ids, w_down, w_down, experts, pair_cap, width // 2, (0, 1))
    raw_down = exchange(after(packed_down, raw), experts)

    gate_up_rows = unpack_two(raw, pair_cap)
    part = product(rows_x, gate_up_rows, True)
    sent_grads = dispatch(route, score, cotangent, experts, tok_cap, True)
    rows_dy = exchange(after(sent_grads, (raw_down, part)), experts)
    hidden, sums = hidden_of(scatter_sum(part))
    hidden = gather_blocks(hidden)
    down_rows = unpack_one(raw_down, pair_cap)
    out_part = product(hidden, down_rows, False)
    out_part, rows_dy = lax.optimization_barrier((out_part, rows_dy))
    back_out = exchange(out_part, experts)

    back = scatter_sum(product(rows_dy, down_rows, True))
    d_both = gather_blocks(backprop_of(back, sums))
    input_part = product(d_both, gate_up_rows, False)
    back_in = exchange(after(input_part, back_out), experts)

    d_both, hidden, rows_dy = after((d_both, hidden, rows_dy), input_part)
    grad_down = lax.dot_general(hidden, rows_dy, over_rows, preferred_element_type=F32)
    grad_gate = lax.dot_general(
        d_both[:, :SLOTS], rows_x, over_rows, preferred_element_type=F32
    )
    grad_up = lax.dot_general(d_both[:, SLOTS:], rows_x, over_rows, preferred_element_type=F32)
    mixed = combine(route, score, back_out, experts, tok_cap, True)
    input_grad = combine(route, score, back_in, experts, tok_cap, False)
    return (
        mixed,
        input_grad,
        grad_gate.astype(BF16)[None],
        grad_up.astype(BF16)[None],
        grad_down.astype(BF16)[None],
    )


def solution(mesh):
    fine = Mesh(mesh.devices.reshape(4, 2, 8, 4), DP + EXPERT)
    full, rows_only = P(EXPERT, DP), P(EXPERT, None)
    grads = P(EXPERT, None, DP)
    return jax.shard_map(
        body,
        mesh=fine,
        in_specs=(full, full, rows_only, rows_only, rows_only, full, full, full),
        out_specs=(full, full, grads, grads, grads),
        check_vma=False,
    )
```

```python
import functools

import jax
import jax.numpy as jnp
from jax import lax
from jax.experimental import pallas as pl
from jax.experimental.pallas import tpu as pltpu
from jax.sharding import Mesh
from jax.sharding import PartitionSpec as P

SLOTS = 640
EXPERT = ("z", "x")
DP = ("y", "core")
BF16 = jnp.bfloat16
F32 = jnp.float32
LIMIT = 48 * 1024 * 1024
NOTE = 16
FREE = pl.CostEstimate(flops=0, bytes_accessed=0, transcendentals=0)


def iota(shape, axis):
    return lax.broadcasted_iota(jnp.int32, shape, axis)


def kernel_call(body, name, **kwargs):
    return pl.pallas_call(
        body,
        name=name,
        compiler_params=pltpu.CompilerParams(vmem_limit_bytes=LIMIT),
        **kwargs,
    )


def ranks(rows, count):
    n = rows[0].shape[1]
    hits = [iota((count, n), 0) == ids for ids in rows]
    seen = sum(hit.astype(F32) for hit in hits).astype(BF16)
    earlier = (iota((n, n), 0) < iota((n, n), 1)).astype(F32).astype(BF16)
    before = jnp.dot(seen, earlier, preferred_element_type=F32)
    return [
        jnp.sum(jnp.where(hit, before, 0.0), axis=0, keepdims=True).astype(jnp.int32)
        for hit in hits
    ]


def token_places(route_ref, experts, cap):
    rows = [route_ref[0:1, :], route_ref[1:2, :]]
    return [ids * cap + rank for ids, rank in zip(rows, ranks(rows, experts))]


def token_shares(score_ref):
    score = score_ref[...].astype(F32)
    first, second = score[0:1, :], score[1:2, :]
    total = first + second
    return first / total, second / total


def announce_body(route_ref, score_ref, x_ref, out_ref):
    count = x_ref.shape[0]
    out_ref[0:count, :] = x_ref[...]
    rows = out_ref.shape[0] - count
    for k in (0, 1):
        ids = route_ref[k : k + 1, :].astype(F32).astype(BF16)
        points = score_ref[k : k + 1, :].astype(F32).astype(BF16)
        out_ref[count:, k * count : (k + 1) * count] = jnp.broadcast_to(ids, (rows, count))
        out_ref[count:, (k + 2) * count : (k + 3) * count] = jnp.broadcast_to(
            points, (rows, count)
        )


def announce(route, score, x):
    count, width = x.shape
    return kernel_call(
        announce_body,
        "announce",
        out_shape=jax.ShapeDtypeStruct((count + NOTE, width), BF16),
        cost_estimate=FREE,
    )(route, score, x)


def sort_body(scaled, experts, cap, sources, far, at_ref, *refs):
    lanes = lax.axis_size("x")
    ins, outs = refs[:-lanes], refs[-lanes:]
    base, column = at_ref[0] * lanes, at_ref[1]
    used = 0
    for k in range(sources):
        pieces = 2 if far and k == sources - 1 else 1
        note_refs = ins[used : used + pieces]
        used += pieces
        x_refs = note_refs
        if scaled:
            x_refs = ins[used : used + pieces]
            used += pieces
        count = note_refs[0].shape[0] - NOTE
        note = [ref[count:, :].astype(F32)[0:1, :] for ref in note_refs]
        note = note[0] if pieces == 1 else jnp.concatenate(note, axis=1)
        ids = [note[:, i * count : (i + 1) * count].astype(jnp.int32) for i in (0, 1)]
        slot = iota((lanes * cap, count), 0)
        hits = []
        for own, rank in zip(ids, ranks(ids, experts)):
            there = own - base
            inside = (there >= 0) & (there < lanes)
            step = (there - column + lanes) % lanes
            hits.append(slot == jnp.where(inside, step * cap + rank, -1))
        picks = jnp.where(hits[0] | hits[1], 1.0, 0.0).astype(BF16)
        if scaled:
            first, second = (note[:, i * count : (i + 1) * count] for i in (2, 3))
            total = first + second
            weight = jnp.where(hits[0], first / total, 0.0) + jnp.where(
                hits[1], second / total, 0.0
            )
            weight = jnp.sum(weight, axis=1, keepdims=True)
        start = 0
        for ref in x_refs:
            rows = jnp.dot(picks, ref[0:count, :], preferred_element_type=F32)
            if scaled:
                rows = rows * weight
            rows = rows.astype(BF16)
            width = ref.shape[1]
            for step, out in enumerate(outs):
                out[k * cap : (k + 1) * cap, start : start + width] = rows[
                    step * cap : (step + 1) * cap, :
                ]
            start += width


def sort_rows(notes, data, at, experts, cap, far, width):
    lanes = lax.axis_size("x")
    scaled = data is not None
    operands = []
    for k, note in enumerate(notes):
        operands += note
        if scaled:
            operands += data[k]
    vmem = pl.BlockSpec(memory_space=pltpu.VMEM)
    shape = jax.ShapeDtypeStruct((len(notes) * cap, width), BF16)
    return kernel_call(
        functools.partial(sort_body, scaled, experts, cap, len(notes), far),
        "sort_rows",
        in_specs=[pl.BlockSpec(memory_space=pltpu.SMEM)] + [vmem] * len(operands),
        out_specs=[vmem] * lanes,
        out_shape=[shape] * lanes,
        cost_estimate=FREE,
    )(at, *operands)


def assemble_body(cap, steps, at_ref, *refs):
    lanes, planes = lax.axis_size("x"), lax.axis_size("z")
    out_ref = refs[-1]
    z, x = at_ref[0], at_ref[1]
    for group, offsets in enumerate(steps):
        for step in range(lanes):
            ref = refs[group * lanes + step]
            for k, offset in enumerate(offsets):
                source = lax.rem(z + planes - offset, planes) * lanes + lax.rem(
                    x + lanes - step, lanes
                )
                start = pl.multiple_of(source * cap, cap)
                out_ref[pl.ds(start, cap), :] = ref[k * cap : (k + 1) * cap, :]


def assemble(groups, steps, at, experts, cap):
    arrays = [array for group in groups for array in group]
    vmem = pl.BlockSpec(memory_space=pltpu.VMEM)
    return kernel_call(
        functools.partial(assemble_body, cap, steps),
        "assemble",
        in_specs=[pl.BlockSpec(memory_space=pltpu.SMEM)] + [vmem] * len(arrays),
        out_specs=vmem,
        out_shape=jax.ShapeDtypeStruct((experts * cap, arrays[0].shape[1]), BF16),
        cost_estimate=FREE,
    )(at, *arrays)


NEAR = (0, 1, -1, 2, -2)
FAR = (3, -3, 4)


def around(value):
    half = value.shape[1] // 2
    held = {0: [value]}
    for step in (1, 2, 3):
        held[step] = [shift(held[step - 1][0], "z", 1)]
        held[-step] = [shift(held[1 - step][0], "z", -1)]
    held[4] = [
        shift(held[3][0][:, :half], "z", 1),
        shift(held[-3][0][:, half:], "z", -1),
    ]
    return held


def deliver(notes, data, at, experts, cap, width):
    groups = []
    for steps in (NEAR, FAR):
        sent = sort_rows(
            [notes[step] for step in steps],
            None if data is None else [data[step] for step in steps],
            at,
            experts,
            cap,
            4 in steps,
            width,
        )
        groups.append(
            [rows if step == 0 else shift(rows, "x", step) for step, rows in enumerate(sent)]
        )
    return assemble(groups, (NEAR, FAR), at, experts, cap)


def pack_body(experts, cap, ids_ref, a_ref, b_ref, out_ref):
    block, count = out_ref.shape[0], a_ref.shape[0]
    ids = ids_ref[...]
    place = ids * (2 * cap) + ranks([ids], experts)[0]
    slot = iota((block, count), 0) + pl.program_id(0) * block
    pick_a = jnp.where(slot == place, 1.0, 0.0).astype(BF16)
    pick_b = jnp.where(slot == place + cap, 1.0, 0.0).astype(BF16)
    out_ref[...] = (
        jnp.dot(pick_a, a_ref[...], preferred_element_type=F32)
        + jnp.dot(pick_b, b_ref[...], preferred_element_type=F32)
    ).astype(BF16)


def pack(ids, a, b, experts, cap, width, columns):
    count = a.shape[0]
    block = 256
    total = 2 * experts * cap
    whole = lambda i: (0, 0)
    return kernel_call(
        functools.partial(pack_body, experts, cap),
        "pack",
        grid=(total // block,),
        in_specs=[
            pl.BlockSpec((1, count), whole),
            pl.BlockSpec((count, width), lambda i: (0, columns[0])),
            pl.BlockSpec((count, width), lambda i: (0, columns[1])),
        ],
        out_specs=pl.BlockSpec((block, width), lambda i: (i, 0)),
        out_shape=jax.ShapeDtypeStruct((total, width), BF16),
    )(ids, a, b)


def unpack_picks(block, cap):
    row, column = iota((block, 2 * block), 0), iota((block, 2 * block), 1)
    group = sum((row >= g * cap).astype(jnp.int32) for g in range(1, block // cap))
    first = row + cap * group
    return [jnp.where(column == first + k * cap, 1.0, 0.0).astype(BF16) for k in (0, 1)]


def unpack_two_body(cap, raw_ref, out_ref):
    picks = unpack_picks(out_ref.shape[1], cap)
    raw = raw_ref[...]
    for k in (0, 1):
        out_ref[k] = jnp.dot(picks[k], raw, preferred_element_type=F32).astype(BF16)


def unpack_one_body(cap, raw_ref, out_ref):
    width = raw_ref.shape[1]
    picks = unpack_picks(out_ref.shape[0], cap)
    raw = raw_ref[...]
    for k in (0, 1):
        out_ref[:, k * width : (k + 1) * width] = jnp.dot(
            picks[k], raw, preferred_element_type=F32
        ).astype(BF16)


def unpack_two(raw, cap):
    rows, width = raw.shape[0] // 2, raw.shape[1]
    block = 160
    return kernel_call(
        functools.partial(unpack_two_body, cap),
        "unpack_two",
        grid=(rows // block,),
        in_specs=[pl.BlockSpec((2 * block, width), lambda i: (i, 0))],
        out_specs=pl.BlockSpec((2, block, width), lambda i: (0, i, 0)),
        out_shape=jax.ShapeDtypeStruct((2, rows, width), BF16),
    )(raw).reshape(2 * rows, width)


def unpack_one(raw, cap):
    rows, width = raw.shape[0] // 2, raw.shape[1]
    block = 160
    return kernel_call(
        functools.partial(unpack_one_body, cap),
        "unpack_one",
        grid=(rows // block,),
        in_specs=[pl.BlockSpec((2 * block, width), lambda i: (i, 0))],
        out_specs=pl.BlockSpec((block, 2 * width), lambda i: (i, 0)),
        out_shape=jax.ShapeDtypeStruct((rows, 2 * width), BF16),
    )(raw)


def add_half_body(start, rows_ref, half_ref, out_ref):
    width = half_ref.shape[1]
    out_ref[...] = rows_ref[...]
    side = (slice(None), slice(start, start + width))
    out_ref[side] = (rows_ref[side].astype(F32) + half_ref[...].astype(F32)).astype(BF16)


def add_half(rows, half, start):
    return kernel_call(
        functools.partial(add_half_body, start),
        "add_half",
        out_shape=jax.ShapeDtypeStruct(rows.shape, BF16),
        cost_estimate=FREE,
    )(rows, half)


def sum_three(refs):
    return sum(ref[...].astype(F32) for ref in refs)


def hidden_body(own_ref, below_ref, above_ref, hidden_ref, sums_ref):
    sums = sum_three((own_ref, below_ref, above_ref))
    sums_ref[...] = sums
    hidden_ref[...] = activate(sums[:, :SLOTS], sums[:, SLOTS:])


def hidden_of(parts):
    rows, n = parts[0].shape
    return kernel_call(
        hidden_body,
        "hidden",
        out_shape=[
            jax.ShapeDtypeStruct((rows, n // 2), BF16),
            jax.ShapeDtypeStruct((rows, n), F32),
        ],
        cost_estimate=FREE,
    )(*parts)


def backprop_body(own_ref, below_ref, above_ref, sums_ref, out_ref):
    back = sum_three((own_ref, below_ref, above_ref))
    d_gate, d_up = backprop(back, sums_ref[:, :SLOTS], sums_ref[:, SLOTS:])
    out_ref[:, :SLOTS] = d_gate
    out_ref[:, SLOTS:] = d_up


def backprop_of(parts, sums):
    return kernel_call(
        backprop_body,
        "backprop",
        out_shape=jax.ShapeDtypeStruct(sums.shape, BF16),
        cost_estimate=FREE,
    )(*parts, sums)


def interleave_body(core_ref, own_ref, other_ref, out_ref):
    core = core_ref[0]
    out_ref[:, core] = own_ref[...]
    out_ref[:, 1 - core] = other_ref[...]


def interleave(own, other, core):
    ys, rows, n = own.shape
    return kernel_call(
        interleave_body,
        "interleave",
        in_specs=[
            pl.BlockSpec(memory_space=pltpu.SMEM),
            pl.BlockSpec(memory_space=pltpu.VMEM),
            pl.BlockSpec(memory_space=pltpu.VMEM),
        ],
        out_shape=jax.ShapeDtypeStruct((ys, 2, rows, n), own.dtype),
        cost_estimate=FREE,
    )(core[None], own, other)


def product_body(dims, a_ref, b_ref, out_ref):
    out_ref[...] = lax.dot_general(
        a_ref[...], b_ref[...], dims, preferred_element_type=F32
    ).astype(BF16)


def product(a, b, transposed):
    rows, depth = a.shape
    n = b.shape[0 if transposed else 1]
    block = 256
    dims = (((1,), (1 if transposed else 0,)), ((), ()))
    return kernel_call(
        functools.partial(product_body, dims),
        "product",
        grid=(rows // block,),
        in_specs=[
            pl.BlockSpec((block, depth), lambda i: (i, 0)),
            pl.BlockSpec(b.shape, lambda i: (0, 0)),
        ],
        out_specs=pl.BlockSpec((block, n), lambda i: (i, 0)),
        out_shape=jax.ShapeDtypeStruct((rows, n), BF16),
        cost_estimate=FREE,
    )(a, b)


def column_of(row):
    n = row.shape[1]
    same = iota((n, n), 0) == iota((n, n), 1)
    return jnp.sum(jnp.where(same, row, jnp.zeros_like(row)), axis=1, keepdims=True)


def combine_body(scaled, experts, cap, *refs):
    route_ref, rows_ref, out_ref = refs[0], refs[-2], refs[-1]
    count, total = out_ref.shape[0], rows_ref.shape[0]
    places = [column_of(place) for place in token_places(route_ref, experts, cap)]
    slot = iota((count, total), 1)
    hits = [slot == place for place in places]
    rows = rows_ref[...]
    if scaled:
        shares = [column_of(share) for share in token_shares(refs[1])]
        weight = jnp.where(hits[0], shares[0], 0.0) + jnp.where(hits[1], shares[1], 0.0)
        high = weight.astype(BF16)
        low = (weight - high.astype(F32)).astype(BF16)
        total_rows = jnp.dot(high, rows, preferred_element_type=F32) + jnp.dot(
            low, rows, preferred_element_type=F32
        )
    else:
        pick = jnp.where(hits[0] | hits[1], 1.0, 0.0).astype(BF16)
        total_rows = jnp.dot(pick, rows, preferred_element_type=F32)
    out_ref[...] = total_rows.astype(BF16)


def combine(route, score, rows, experts, cap, scaled):
    count = route.shape[1]
    total, width = rows.shape
    block = 512
    whole = lambda i: (0, 0)
    return kernel_call(
        functools.partial(combine_body, scaled, experts, cap),
        "combine",
        grid=(width // block,),
        in_specs=[pl.BlockSpec((2, count), whole)] * (2 if scaled else 1)
        + [pl.BlockSpec((total, block), lambda i: (0, i))],
        out_specs=pl.BlockSpec((count, block), lambda i: (0, i)),
        out_shape=jax.ShapeDtypeStruct((count, width), BF16),
    )(*((route, score) if scaled else (route,)), rows)


def exchange(rows, parts):
    total, width = rows.shape
    return lax.all_to_all(
        rows.reshape(parts, total // parts, width),
        EXPERT,
        split_axis=0,
        concat_axis=0,
        tiled=True,
    ).reshape(total, width)


def after(value, other):
    return lax.optimization_barrier((value, other))[0]


def shift(value, axis, step):
    size = lax.axis_size(axis)
    return lax.ppermute(value, axis, [(i, (i + step) % size) for i in range(size)])


def pick(value, index, axis):
    return lax.dynamic_index_in_dim(value, index, axis, keepdims=False)


def put(value, part, y, core):
    return lax.dynamic_update_slice(value, part[None, None], (y, core, 0, 0))


def scatter_sum(value):
    rows, n = value.shape
    ys, cores = lax.axis_size("y"), lax.axis_size("core")
    y, core = lax.axis_index("y"), lax.axis_index("core")
    value = value.reshape(ys, cores, rows // (ys * cores), n)
    other = shift(pick(value, 1 - core, 1), "core", 1)
    pair = (pick(value, core, 1).astype(F32) + other.astype(F32)).astype(BF16)
    half = n // 256 * 128
    far = pick(pair, (y + 2) % ys, 0)
    low = shift(far[:, :half], "y", 1)
    high = shift(far[:, half:], "y", -1)
    to_above = add_half(pick(pair, (y + 1) % ys, 0), low, 0)
    to_below = add_half(pick(pair, (y + ys - 1) % ys, 0), high, half)
    return pick(pair, y, 0), shift(to_above, "y", 1), shift(to_below, "y", -1)


def gather_blocks(part):
    rows, n = part.shape
    ys, cores = lax.axis_size("y"), lax.axis_size("core")
    y, core = lax.axis_index("y"), lax.axis_index("core")
    half = n // 256 * 128
    from_below = shift(part, "y", 1)
    from_above = shift(part, "y", -1)
    low = shift(from_below[:, :half], "y", 1)
    high = shift(from_above[:, half:], "y", -1)
    far = jnp.concatenate([low, high], axis=1)
    column = jnp.zeros((ys, rows, n), part.dtype)
    for k, piece in enumerate((part, from_below, far, from_above)):
        column = lax.dynamic_update_slice(column, piece[None], ((y + ys - k) % ys, 0, 0))
    other = shift(column, "core", 1)
    return interleave(column, other, core).reshape(ys * cores * rows, n)


def activate(gate, upper):
    sig = jax.nn.sigmoid(gate)
    return (gate * sig * upper).astype(BF16)


def backprop(back, gate, upper):
    sig = jax.nn.sigmoid(gate)
    d_gate = (back * upper * sig * (1.0 + gate * (1.0 - sig))).astype(BF16)
    d_up = (back * gate * sig).astype(BF16)
    return d_gate, d_up


def body(tokens, cotangent, route, score, clusters, w_gate, w_up, w_down):
    experts = lax.axis_size(EXPERT)
    pair_cap = SLOTS // experts
    tok_count, width = tokens.shape
    tok_cap = 4 * tok_count // experts
    route, score, ids = route.T, score.T, clusters.T
    over_rows = (((0,), (0,)), ((), ()))

    at = jnp.stack([lax.axis_index("z"), lax.axis_index("x")])
    notes = around(announce(route, score, tokens))
    packed = pack(ids, w_gate, w_up, experts, pair_cap, width, (0, 0))
    raw = exchange(packed, experts)
    rows_x = deliver(notes, None, at, experts, tok_cap, width)
    raw, rows_x, cotangent = lax.optimization_barrier((raw, rows_x, cotangent))
    packed_down = pack(ids, w_down, w_down, experts, pair_cap, width // 2, (0, 1))
    raw_down = exchange(after(packed_down, raw), experts)
    grads = around(cotangent)

    gate_up_rows = unpack_two(raw, pair_cap)
    part = product(rows_x, gate_up_rows, True)
    hidden, sums = hidden_of(scatter_sum(part))
    hidden = gather_blocks(hidden)
    down_rows = unpack_one(raw_down, pair_cap)
    out_part = product(hidden, down_rows, False)
    back_out = exchange(out_part, experts)
    rows_dy = deliver(notes, grads, at, experts, tok_cap, width)

    back = scatter_sum(product(rows_dy, down_rows, True))
    d_both = gather_blocks(backprop_of(back, sums))
    input_part = product(d_both, gate_up_rows, False)
    back_in = exchange(after(input_part, back_out), experts)

    d_both, hidden, rows_dy = after((d_both, hidden, rows_dy), input_part)
    grad_down = lax.dot_general(hidden, rows_dy, over_rows, preferred_element_type=F32)
    grad_gate = lax.dot_general(
        d_both[:, :SLOTS], rows_x, over_rows, preferred_element_type=F32
    )
    grad_up = lax.dot_general(d_both[:, SLOTS:], rows_x, over_rows, preferred_element_type=F32)
    mixed = combine(route, score, back_out, experts, tok_cap, True)
    input_grad = combine(route, score, back_in, experts, tok_cap, False)
    return (
        mixed,
        input_grad,
        grad_gate.astype(BF16)[None],
        grad_up.astype(BF16)[None],
        grad_down.astype(BF16)[None],
    )


def solution(mesh):
    fine = Mesh(mesh.devices.reshape(4, 2, 8, 4), DP + EXPERT)
    full, rows_only = P(EXPERT, DP), P(EXPERT, None)
    grads = P(EXPERT, None, DP)
    return jax.shard_map(
        body,
        mesh=fine,
        in_specs=(full, full, rows_only, rows_only, rows_only, full, full, full),
        out_specs=(full, full, grads, grads, grads),
        check_vma=False,
    )
```

```python
import functools

import jax
import jax.numpy as jnp
from jax import lax
from jax.experimental import pallas as pl
from jax.experimental.pallas import tpu as pltpu
from jax.sharding import Mesh
from jax.sharding import PartitionSpec as P

SLOTS = 640
EXPERT = ("z", "x")
DP = ("y", "core")
BF16 = jnp.bfloat16
F32 = jnp.float32
LIMIT = 48 * 1024 * 1024
NOTE = 16
FREE = pl.CostEstimate(flops=0, bytes_accessed=0, transcendentals=0)


def iota(shape, axis):
    return lax.broadcasted_iota(jnp.int32, shape, axis)


def kernel_call(body, name, **kwargs):
    return pl.pallas_call(
        body,
        name=name,
        compiler_params=pltpu.CompilerParams(vmem_limit_bytes=LIMIT),
        **kwargs,
    )


def ranks(rows, count):
    n = rows[0].shape[1]
    hits = [iota((count, n), 0) == ids for ids in rows]
    seen = sum(hit.astype(F32) for hit in hits).astype(BF16)
    earlier = (iota((n, n), 0) < iota((n, n), 1)).astype(F32).astype(BF16)
    before = jnp.dot(seen, earlier, preferred_element_type=F32)
    return [
        jnp.sum(jnp.where(hit, before, 0.0), axis=0, keepdims=True).astype(jnp.int32)
        for hit in hits
    ]


def token_places(route_ref, experts, cap):
    rows = [route_ref[0:1, :], route_ref[1:2, :]]
    return [ids * cap + rank for ids, rank in zip(rows, ranks(rows, experts))]


def token_shares(score_ref):
    score = score_ref[...].astype(F32)
    first, second = score[0:1, :], score[1:2, :]
    total = first + second
    return first / total, second / total


def announce_body(route_ref, score_ref, x_ref, out_ref):
    count = x_ref.shape[0]
    out_ref[0:count, :] = x_ref[...]
    rows = out_ref.shape[0] - count
    for k in (0, 1):
        ids = route_ref[k : k + 1, :].astype(F32).astype(BF16)
        points = score_ref[k : k + 1, :].astype(F32).astype(BF16)
        out_ref[count:, k * count : (k + 1) * count] = jnp.broadcast_to(ids, (rows, count))
        out_ref[count:, (k + 2) * count : (k + 3) * count] = jnp.broadcast_to(
            points, (rows, count)
        )


def announce(route, score, x):
    count, width = x.shape
    return kernel_call(
        announce_body,
        "announce",
        out_shape=jax.ShapeDtypeStruct((count + NOTE, width), BF16),
        cost_estimate=FREE,
    )(route, score, x)


def sort_body(scaled, experts, cap, sources, far, at_ref, *refs):
    lanes = lax.axis_size("x")
    ins, outs = refs[:-lanes], refs[-lanes:]
    base, column = at_ref[0] * lanes, at_ref[1]
    used = 0
    for k in range(sources):
        pieces = 2 if far and k == sources - 1 else 1
        note_refs = ins[used : used + pieces]
        used += pieces
        x_refs = note_refs
        if scaled:
            x_refs = ins[used : used + pieces]
            used += pieces
        count = note_refs[0].shape[0] - NOTE
        note = [ref[count:, :].astype(F32)[0:1, :] for ref in note_refs]
        note = note[0] if pieces == 1 else jnp.concatenate(note, axis=1)
        ids = [note[:, i * count : (i + 1) * count].astype(jnp.int32) for i in (0, 1)]
        slot = iota((lanes * cap, count), 0)
        hits = []
        for own, rank in zip(ids, ranks(ids, experts)):
            there = own - base
            inside = (there >= 0) & (there < lanes)
            step = (there - column + lanes) % lanes
            hits.append(slot == jnp.where(inside, step * cap + rank, -1))
        picks = jnp.where(hits[0] | hits[1], 1.0, 0.0).astype(BF16)
        if scaled:
            first, second = (note[:, i * count : (i + 1) * count] for i in (2, 3))
            total = first + second
            weight = jnp.where(hits[0], first / total, 0.0) + jnp.where(
                hits[1], second / total, 0.0
            )
            weight = jnp.sum(weight, axis=1, keepdims=True)
        start = 0
        for ref in x_refs:
            rows = jnp.dot(picks, ref[0:count, :], preferred_element_type=F32)
            if scaled:
                rows = rows * weight
            rows = rows.astype(BF16)
            width = ref.shape[1]
            for step, out in enumerate(outs):
                out[k * cap : (k + 1) * cap, start : start + width] = rows[
                    step * cap : (step + 1) * cap, :
                ]
            start += width


def sort_rows(notes, data, at, experts, cap, far, width):
    lanes = lax.axis_size("x")
    scaled = data is not None
    operands = []
    for k, note in enumerate(notes):
        operands += note
        if scaled:
            operands += data[k]
    vmem = pl.BlockSpec(memory_space=pltpu.VMEM)
    shape = jax.ShapeDtypeStruct((len(notes) * cap, width), BF16)
    return kernel_call(
        functools.partial(sort_body, scaled, experts, cap, len(notes), far),
        "sort_rows",
        in_specs=[pl.BlockSpec(memory_space=pltpu.SMEM)] + [vmem] * len(operands),
        out_specs=[vmem] * lanes,
        out_shape=[shape] * lanes,
        cost_estimate=FREE,
    )(at, *operands)


def assemble_body(cap, steps, at_ref, *refs):
    lanes, planes = lax.axis_size("x"), lax.axis_size("z")
    out_ref = refs[-1]
    z, x = at_ref[0], at_ref[1]
    for group, offsets in enumerate(steps):
        for step in range(lanes):
            ref = refs[group * lanes + step]
            for k, offset in enumerate(offsets):
                source = lax.rem(z + planes - offset, planes) * lanes + lax.rem(
                    x + lanes - step, lanes
                )
                start = pl.multiple_of(source * cap, cap)
                out_ref[pl.ds(start, cap), :] = ref[k * cap : (k + 1) * cap, :]


def assemble(groups, steps, at, experts, cap):
    arrays = [array for group in groups for array in group]
    vmem = pl.BlockSpec(memory_space=pltpu.VMEM)
    return kernel_call(
        functools.partial(assemble_body, cap, steps),
        "assemble",
        in_specs=[pl.BlockSpec(memory_space=pltpu.SMEM)] + [vmem] * len(arrays),
        out_specs=vmem,
        out_shape=jax.ShapeDtypeStruct((experts * cap, arrays[0].shape[1]), BF16),
        cost_estimate=FREE,
    )(at, *arrays)


NEAR = (0, 1, -1, 2, -2)
FAR = (3, -3, 4)


def first_hops(value):
    return [shift(value, "z", 1)], [shift(value, "z", -1)]


def next_hops(up, down):
    return [shift(up[0], "z", 1)], [shift(down[0], "z", -1)]


def last_hops(up, down):
    half = up[0].shape[1] // 2
    return [shift(up[0][:, :half], "z", 1), shift(down[0][:, half:], "z", -1)]


def held_rows(own, hops, last):
    held = {0: [own], 4: last}
    for step, (up, down) in enumerate(hops):
        held[step + 1], held[-step - 1] = up, down
    return held


def deliver(notes, data, at, experts, cap, width):
    groups = []
    for steps in (NEAR, FAR):
        sent = sort_rows(
            [notes[step] for step in steps],
            None if data is None else [data[step] for step in steps],
            at,
            experts,
            cap,
            4 in steps,
            width,
        )
        groups.append(
            [rows if step == 0 else shift(rows, "x", step) for step, rows in enumerate(sent)]
        )
    return assemble(groups, (NEAR, FAR), at, experts, cap)


def pack_body(experts, cap, ids_ref, a_ref, b_ref, out_ref):
    block, count = out_ref.shape[0], a_ref.shape[0]
    ids = ids_ref[...]
    place = ids * (2 * cap) + ranks([ids], experts)[0]
    slot = iota((block, count), 0) + pl.program_id(0) * block
    pick_a = jnp.where(slot == place, 1.0, 0.0).astype(BF16)
    pick_b = jnp.where(slot == place + cap, 1.0, 0.0).astype(BF16)
    out_ref[...] = (
        jnp.dot(pick_a, a_ref[...], preferred_element_type=F32)
        + jnp.dot(pick_b, b_ref[...], preferred_element_type=F32)
    ).astype(BF16)


def pack(ids, a, b, experts, cap, width, columns):
    count = a.shape[0]
    block = 256
    total = 2 * experts * cap
    whole = lambda i: (0, 0)
    return kernel_call(
        functools.partial(pack_body, experts, cap),
        "pack",
        grid=(total // block,),
        in_specs=[
            pl.BlockSpec((1, count), whole),
            pl.BlockSpec((count, width), lambda i: (0, columns[0])),
            pl.BlockSpec((count, width), lambda i: (0, columns[1])),
        ],
        out_specs=pl.BlockSpec((block, width), lambda i: (i, 0)),
        out_shape=jax.ShapeDtypeStruct((total, width), BF16),
    )(ids, a, b)


def unpack_picks(block, cap):
    row, column = iota((block, 2 * block), 0), iota((block, 2 * block), 1)
    group = sum((row >= g * cap).astype(jnp.int32) for g in range(1, block // cap))
    first = row + cap * group
    return [jnp.where(column == first + k * cap, 1.0, 0.0).astype(BF16) for k in (0, 1)]


def unpack_two_body(cap, raw_ref, out_ref):
    picks = unpack_picks(out_ref.shape[1], cap)
    raw = raw_ref[...]
    for k in (0, 1):
        out_ref[k] = jnp.dot(picks[k], raw, preferred_element_type=F32).astype(BF16)


def unpack_one_body(cap, raw_ref, out_ref):
    width = raw_ref.shape[1]
    picks = unpack_picks(out_ref.shape[0], cap)
    raw = raw_ref[...]
    for k in (0, 1):
        out_ref[:, k * width : (k + 1) * width] = jnp.dot(
            picks[k], raw, preferred_element_type=F32
        ).astype(BF16)


def unpack_two(raw, cap):
    rows, width = raw.shape[0] // 2, raw.shape[1]
    block = 160
    return kernel_call(
        functools.partial(unpack_two_body, cap),
        "unpack_two",
        grid=(rows // block,),
        in_specs=[pl.BlockSpec((2 * block, width), lambda i: (i, 0))],
        out_specs=pl.BlockSpec((2, block, width), lambda i: (0, i, 0)),
        out_shape=jax.ShapeDtypeStruct((2, rows, width), BF16),
    )(raw).reshape(2 * rows, width)


def unpack_one(raw, cap):
    rows, width = raw.shape[0] // 2, raw.shape[1]
    block = 160
    return kernel_call(
        functools.partial(unpack_one_body, cap),
        "unpack_one",
        grid=(rows // block,),
        in_specs=[pl.BlockSpec((2 * block, width), lambda i: (i, 0))],
        out_specs=pl.BlockSpec((block, 2 * width), lambda i: (i, 0)),
        out_shape=jax.ShapeDtypeStruct((rows, 2 * width), BF16),
    )(raw)


def add_half_body(start, rows_ref, half_ref, out_ref):
    width = half_ref.shape[1]
    out_ref[...] = rows_ref[...]
    side = (slice(None), slice(start, start + width))
    out_ref[side] = (rows_ref[side].astype(F32) + half_ref[...].astype(F32)).astype(BF16)


def add_half(rows, half, start):
    return kernel_call(
        functools.partial(add_half_body, start),
        "add_half",
        out_shape=jax.ShapeDtypeStruct(rows.shape, BF16),
        cost_estimate=FREE,
    )(rows, half)


def sum_three(refs):
    return sum(ref[...].astype(F32) for ref in refs)


def hidden_body(own_ref, below_ref, above_ref, hidden_ref, sums_ref):
    sums = sum_three((own_ref, below_ref, above_ref))
    sums_ref[...] = sums
    hidden_ref[...] = activate(sums[:, :SLOTS], sums[:, SLOTS:])


def hidden_of(parts):
    rows, n = parts[0].shape
    return kernel_call(
        hidden_body,
        "hidden",
        out_shape=[
            jax.ShapeDtypeStruct((rows, n // 2), BF16),
            jax.ShapeDtypeStruct((rows, n), F32),
        ],
        cost_estimate=FREE,
    )(*parts)


def backprop_body(own_ref, below_ref, above_ref, sums_ref, out_ref):
    back = sum_three((own_ref, below_ref, above_ref))
    d_gate, d_up = backprop(back, sums_ref[:, :SLOTS], sums_ref[:, SLOTS:])
    out_ref[:, :SLOTS] = d_gate
    out_ref[:, SLOTS:] = d_up


def backprop_of(parts, sums):
    return kernel_call(
        backprop_body,
        "backprop",
        out_shape=jax.ShapeDtypeStruct(sums.shape, BF16),
        cost_estimate=FREE,
    )(*parts, sums)


def interleave_body(core_ref, own_ref, other_ref, out_ref):
    core = core_ref[0]
    out_ref[:, core] = own_ref[...]
    out_ref[:, 1 - core] = other_ref[...]


def interleave(own, other, core):
    ys, rows, n = own.shape
    return kernel_call(
        interleave_body,
        "interleave",
        in_specs=[
            pl.BlockSpec(memory_space=pltpu.SMEM),
            pl.BlockSpec(memory_space=pltpu.VMEM),
            pl.BlockSpec(memory_space=pltpu.VMEM),
        ],
        out_shape=jax.ShapeDtypeStruct((ys, 2, rows, n), own.dtype),
        cost_estimate=FREE,
    )(core[None], own, other)


def product_body(dims, a_ref, b_ref, out_ref):
    out_ref[...] = lax.dot_general(
        a_ref[...], b_ref[...], dims, preferred_element_type=F32
    ).astype(BF16)


def product(a, b, transposed):
    rows, depth = a.shape
    n = b.shape[0 if transposed else 1]
    block = 256
    dims = (((1,), (1 if transposed else 0,)), ((), ()))
    return kernel_call(
        functools.partial(product_body, dims),
        "product",
        grid=(rows // block,),
        in_specs=[
            pl.BlockSpec((block, depth), lambda i: (i, 0)),
            pl.BlockSpec(b.shape, lambda i: (0, 0)),
        ],
        out_specs=pl.BlockSpec((block, n), lambda i: (i, 0)),
        out_shape=jax.ShapeDtypeStruct((rows, n), BF16),
        cost_estimate=FREE,
    )(a, b)


def column_of(row):
    n = row.shape[1]
    same = iota((n, n), 0) == iota((n, n), 1)
    return jnp.sum(jnp.where(same, row, jnp.zeros_like(row)), axis=1, keepdims=True)


def combine_body(scaled, experts, cap, *refs):
    route_ref, rows_ref, out_ref = refs[0], refs[-2], refs[-1]
    count, total = out_ref.shape[0], rows_ref.shape[0]
    places = [column_of(place) for place in token_places(route_ref, experts, cap)]
    slot = iota((count, total), 1)
    hits = [slot == place for place in places]
    rows = rows_ref[...]
    if scaled:
        shares = [column_of(share) for share in token_shares(refs[1])]
        weight = jnp.where(hits[0], shares[0], 0.0) + jnp.where(hits[1], shares[1], 0.0)
        high = weight.astype(BF16)
        low = (weight - high.astype(F32)).astype(BF16)
        total_rows = jnp.dot(high, rows, preferred_element_type=F32) + jnp.dot(
            low, rows, preferred_element_type=F32
        )
    else:
        pick = jnp.where(hits[0] | hits[1], 1.0, 0.0).astype(BF16)
        total_rows = jnp.dot(pick, rows, preferred_element_type=F32)
    out_ref[...] = total_rows.astype(BF16)


def combine(route, score, rows, experts, cap, scaled):
    count = route.shape[1]
    total, width = rows.shape
    block = 512
    whole = lambda i: (0, 0)
    return kernel_call(
        functools.partial(combine_body, scaled, experts, cap),
        "combine",
        grid=(width // block,),
        in_specs=[pl.BlockSpec((2, count), whole)] * (2 if scaled else 1)
        + [pl.BlockSpec((total, block), lambda i: (0, i))],
        out_specs=pl.BlockSpec((count, block), lambda i: (0, i)),
        out_shape=jax.ShapeDtypeStruct((count, width), BF16),
    )(*((route, score) if scaled else (route,)), rows)


def exchange(rows, parts):
    total, width = rows.shape
    return lax.all_to_all(
        rows.reshape(parts, total // parts, width),
        EXPERT,
        split_axis=0,
        concat_axis=0,
        tiled=True,
    ).reshape(total, width)


def after(value, other):
    return lax.optimization_barrier((value, other))[0]


def shift(value, axis, step):
    size = lax.axis_size(axis)
    return lax.ppermute(value, axis, [(i, (i + step) % size) for i in range(size)])


def pick(value, index, axis):
    return lax.dynamic_index_in_dim(value, index, axis, keepdims=False)


def put(value, part, y, core):
    return lax.dynamic_update_slice(value, part[None, None], (y, core, 0, 0))


def chip_sum(value):
    rows, n = value.shape
    ys, cores = lax.axis_size("y"), lax.axis_size("core")
    core = lax.axis_index("core")
    value = value.reshape(ys, cores, rows // (ys * cores), n)
    other = shift(pick(value, 1 - core, 1), "core", 1)
    return (pick(value, core, 1).astype(F32) + other.astype(F32)).astype(BF16)


def scatter_sum(pair):
    ys, n = pair.shape[0], pair.shape[2]
    y = lax.axis_index("y")
    half = n // 256 * 128
    far = pick(pair, (y + 2) % ys, 0)
    low = shift(far[:, :half], "y", 1)
    high = shift(far[:, half:], "y", -1)
    to_above = add_half(pick(pair, (y + 1) % ys, 0), low, 0)
    to_below = add_half(pick(pair, (y + ys - 1) % ys, 0), high, half)
    return pick(pair, y, 0), shift(to_above, "y", 1), shift(to_below, "y", -1)


def gather_blocks(part):
    rows, n = part.shape
    ys, cores = lax.axis_size("y"), lax.axis_size("core")
    y, core = lax.axis_index("y"), lax.axis_index("core")
    half = n // 256 * 128
    from_below = shift(part, "y", 1)
    from_above = shift(part, "y", -1)
    low = shift(from_below[:, :half], "y", 1)
    high = shift(from_above[:, half:], "y", -1)
    far = jnp.concatenate([low, high], axis=1)
    column = jnp.zeros((ys, rows, n), part.dtype)
    for k, piece in enumerate((part, from_below, far, from_above)):
        column = lax.dynamic_update_slice(column, piece[None], ((y + ys - k) % ys, 0, 0))
    other = shift(column, "core", 1)
    return interleave(column, other, core).reshape(ys * cores * rows, n)


def activate(gate, upper):
    sig = jax.nn.sigmoid(gate)
    return (gate * sig * upper).astype(BF16)


def backprop(back, gate, upper):
    sig = jax.nn.sigmoid(gate)
    d_gate = (back * upper * sig * (1.0 + gate * (1.0 - sig))).astype(BF16)
    d_up = (back * gate * sig).astype(BF16)
    return d_gate, d_up


def body(tokens, cotangent, route, score, clusters, w_gate, w_up, w_down):
    experts = lax.axis_size(EXPERT)
    pair_cap = SLOTS // experts
    tok_count, width = tokens.shape
    tok_cap = 4 * tok_count // experts
    route, score, ids = route.T, score.T, clusters.T
    over_rows = (((0,), (0,)), ((), ()))

    at = jnp.stack([lax.axis_index("z"), lax.axis_index("x")])
    noted = announce(route, score, tokens)
    hops = [first_hops(noted)]
    hops.append(next_hops(*hops[-1]))
    hops.append(next_hops(*hops[-1]))
    notes = held_rows(noted, hops, last_hops(*hops[-1]))
    packed = pack(ids, w_gate, w_up, experts, pair_cap, width, (0, 0))
    raw = exchange(after(packed, notes[4]), experts)
    hops = [first_hops(after(cotangent, notes[4]))]
    rows_x = deliver(notes, None, at, experts, tok_cap, width)
    raw, rows_x = lax.optimization_barrier((raw, rows_x))
    gate_up_rows = unpack_two(raw, pair_cap)
    part = product(rows_x, gate_up_rows, True)
    first, part = lax.optimization_barrier((hops[0], part))
    hops.append(next_hops(*first))
    pair = chip_sum(part)
    second, pair = lax.optimization_barrier((hops[1], pair))
    hops.append(next_hops(*second))
    terms = scatter_sum(pair)
    third, terms = lax.optimization_barrier((hops[2], terms))
    grads = held_rows(cotangent, hops, last_hops(*third))
    packed_down = pack(ids, w_down, w_down, experts, pair_cap, width // 2, (0, 1))
    raw_down = exchange(after(packed_down, grads[4]), experts)
    hidden, sums = hidden_of(terms)
    hidden = gather_blocks(hidden)
    down_rows = unpack_one(raw_down, pair_cap)
    out_part = product(hidden, down_rows, False)
    rows_dy = deliver(notes, grads, at, experts, tok_cap, width)
    out_part, rows_dy = lax.optimization_barrier((out_part, rows_dy))
    back_out = exchange(out_part, experts)

    back = scatter_sum(chip_sum(product(rows_dy, down_rows, True)))
    d_both = gather_blocks(backprop_of(back, sums))
    input_part = product(d_both, gate_up_rows, False)
    back_in = exchange(after(input_part, back_out), experts)

    d_both, hidden, rows_dy = after((d_both, hidden, rows_dy), input_part)
    grad_down = lax.dot_general(hidden, rows_dy, over_rows, preferred_element_type=F32)
    grad_gate = lax.dot_general(
        d_both[:, :SLOTS], rows_x, over_rows, preferred_element_type=F32
    )
    grad_up = lax.dot_general(d_both[:, SLOTS:], rows_x, over_rows, preferred_element_type=F32)
    mixed = combine(route, score, back_out, experts, tok_cap, True)
    input_grad = combine(route, score, back_in, experts, tok_cap, False)
    return (
        mixed,
        input_grad,
        grad_gate.astype(BF16)[None],
        grad_up.astype(BF16)[None],
        grad_down.astype(BF16)[None],
    )


def solution(mesh):
    fine = Mesh(mesh.devices.reshape(4, 2, 8, 4), DP + EXPERT)
    full, rows_only = P(EXPERT, DP), P(EXPERT, None)
    grads = P(EXPERT, None, DP)
    return jax.shard_map(
        body,
        mesh=fine,
        in_specs=(full, full, rows_only, rows_only, rows_only, full, full, full),
        out_specs=(full, full, grads, grads, grads),
        check_vma=False,
    )
```

```python
import functools

import jax
import jax.numpy as jnp
from jax import lax
from jax.experimental import pallas as pl
from jax.experimental.pallas import tpu as pltpu
from jax.sharding import Mesh
from jax.sharding import PartitionSpec as P

SLOTS = 640
EXPERT = ("z", "x")
DP = ("y", "core")
BF16 = jnp.bfloat16
F32 = jnp.float32
LIMIT = 48 * 1024 * 1024
FREE = pl.CostEstimate(flops=0, bytes_accessed=0, transcendentals=0)


def iota(shape, axis):
    return lax.broadcasted_iota(jnp.int32, shape, axis)


def kernel_call(body, name, **kwargs):
    return pl.pallas_call(
        body,
        name=name,
        compiler_params=pltpu.CompilerParams(vmem_limit_bytes=LIMIT),
        **kwargs,
    )


def ranks(rows, count):
    n = rows[0].shape[1]
    hits = [iota((count, n), 0) == ids for ids in rows]
    seen = sum(hit.astype(F32) for hit in hits).astype(BF16)
    earlier = (iota((n, n), 0) < iota((n, n), 1)).astype(F32).astype(BF16)
    before = jnp.dot(seen, earlier, preferred_element_type=F32)
    return [
        jnp.sum(jnp.where(hit, before, 0.0), axis=0, keepdims=True).astype(jnp.int32)
        for hit in hits
    ]


def token_places(route_ref, experts, cap):
    rows = [route_ref[0:1, :], route_ref[1:2, :]]
    return [ids * cap + rank for ids, rank in zip(rows, ranks(rows, experts))]


def token_shares(score_ref):
    score = score_ref[...].astype(F32)
    first, second = score[0:1, :], score[1:2, :]
    total = first + second
    return first / total, second / total


def dispatch_body(scaled, experts, cap, *refs):
    route_ref, x_ref, out_ref = refs[0], refs[-2], refs[-1]
    block, count = out_ref.shape[0], x_ref.shape[0]
    places = token_places(route_ref, experts, cap)
    slot = iota((block, count), 0) + pl.program_id(0) * block
    hits = [slot == place for place in places]
    pick = jnp.where(hits[0] | hits[1], 1.0, 0.0).astype(BF16)
    rows = jnp.dot(pick, x_ref[...], preferred_element_type=F32)
    if scaled:
        shares = token_shares(refs[1])
        weight = jnp.where(hits[0], shares[0], 0.0) + jnp.where(hits[1], shares[1], 0.0)
        rows = rows * jnp.sum(weight, axis=1, keepdims=True)
    out_ref[...] = rows.astype(BF16)


def dispatch(route, score, x, experts, cap, scaled):
    count, width = x.shape
    block = 256
    total = experts * cap
    whole = lambda i: (0, 0)
    return kernel_call(
        functools.partial(dispatch_body, scaled, experts, cap),
        "dispatch",
        grid=(total // block,),
        in_specs=[pl.BlockSpec((2, count), whole)] * (2 if scaled else 1)
        + [pl.BlockSpec((count, width), whole)],
        out_specs=pl.BlockSpec((block, width), lambda i: (i, 0)),
        out_shape=jax.ShapeDtypeStruct((total, width), BF16),
    )(*((route, score) if scaled else (route,)), x)


def pack_body(experts, cap, ids_ref, a_ref, b_ref, out_ref):
    block, count = out_ref.shape[0], a_ref.shape[0]
    ids = ids_ref[...]
    place = ids * (2 * cap) + ranks([ids], experts)[0]
    slot = iota((block, count), 0) + pl.program_id(0) * block
    pick_a = jnp.where(slot == place, 1.0, 0.0).astype(BF16)
    pick_b = jnp.where(slot == place + cap, 1.0, 0.0).astype(BF16)
    out_ref[...] = (
        jnp.dot(pick_a, a_ref[...], preferred_element_type=F32)
        + jnp.dot(pick_b, b_ref[...], preferred_element_type=F32)
    ).astype(BF16)


def pack(ids, a, b, experts, cap, width, columns):
    count = a.shape[0]
    block = 256
    total = 2 * experts * cap
    whole = lambda i: (0, 0)
    return kernel_call(
        functools.partial(pack_body, experts, cap),
        "pack",
        grid=(total // block,),
        in_specs=[
            pl.BlockSpec((1, count), whole),
            pl.BlockSpec((count, width), lambda i: (0, columns[0])),
            pl.BlockSpec((count, width), lambda i: (0, columns[1])),
        ],
        out_specs=pl.BlockSpec((block, width), lambda i: (i, 0)),
        out_shape=jax.ShapeDtypeStruct((total, width), BF16),
    )(ids, a, b)


def load_body(experts, cap, pair_cap, route_ref, ids_ref, x_ref, a_ref, b_ref, out_ref):
    per = out_ref.shape[0]
    first = pl.program_id(0) * per
    places = token_places(route_ref, experts, cap)
    slot = iota((per * cap, x_ref.shape[0]), 0) + first * cap
    pick = jnp.where((slot == places[0]) | (slot == places[1]), 1.0, 0.0).astype(BF16)
    tokens = jnp.dot(pick, x_ref[...], preferred_element_type=F32)
    ids, pairs = ids_ref[...], 2 * pair_cap
    place = ids * pairs + ranks([ids], experts)[0]
    slot = iota((per * pairs, a_ref.shape[0]), 0) + first * pairs
    pick_a = jnp.where(slot == place, 1.0, 0.0).astype(BF16)
    pick_b = jnp.where(slot == place + pair_cap, 1.0, 0.0).astype(BF16)
    weights = jnp.dot(pick_a, a_ref[...], preferred_element_type=F32) + jnp.dot(
        pick_b, b_ref[...], preferred_element_type=F32
    )
    for k in range(per):
        out_ref[k, :cap, :] = tokens[k * cap : (k + 1) * cap, :].astype(BF16)
        out_ref[k, cap:, :] = weights[k * pairs : (k + 1) * pairs, :].astype(BF16)


def load(route, ids, x, a, b, experts, cap, pair_cap):
    width = x.shape[1]
    per = 4
    whole = lambda i: (0, 0)
    return kernel_call(
        functools.partial(load_body, experts, cap, pair_cap),
        "load",
        grid=(experts // per,),
        in_specs=[pl.BlockSpec(v.shape, whole) for v in (route, ids, x, a, b)],
        out_specs=pl.BlockSpec((per, cap + 2 * pair_cap, width), lambda i: (i, 0, 0)),
        out_shape=jax.ShapeDtypeStruct((experts, cap + 2 * pair_cap, width), BF16),
    )(route, ids, x, a, b)


def unload_body(cap, pair_cap, raw_ref, rows_ref, weights_ref):
    per = raw_ref.shape[0]
    for k in range(per):
        rows_ref[k * cap : (k + 1) * cap, :] = raw_ref[k, :cap, :]
    raw = jnp.concatenate(
        [raw_ref[k, cap:, :].astype(F32) for k in range(per)], axis=0
    ).astype(BF16)
    picks = unpack_picks(weights_ref.shape[1], pair_cap)
    for k in (0, 1):
        weights_ref[k] = jnp.dot(picks[k], raw, preferred_element_type=F32).astype(BF16)


def unload(raw, cap, pair_cap):
    experts, width = raw.shape[0], raw.shape[2]
    per = 8
    rows, weights = kernel_call(
        functools.partial(unload_body, cap, pair_cap),
        "unload",
        grid=(experts // per,),
        in_specs=[pl.BlockSpec((per,) + raw.shape[1:], lambda i: (i, 0, 0))],
        out_specs=[
            pl.BlockSpec((per * cap, width), lambda i: (i, 0)),
            pl.BlockSpec((2, per * pair_cap, width), lambda i: (0, i, 0)),
        ],
        out_shape=[
            jax.ShapeDtypeStruct((experts * cap, width), BF16),
            jax.ShapeDtypeStruct((2, experts * pair_cap, width), BF16),
        ],
    )(raw)
    return rows, weights.reshape(2 * experts * pair_cap, width)


def unpack_picks(block, cap):
    row, column = iota((block, 2 * block), 0), iota((block, 2 * block), 1)
    group = sum((row >= g * cap).astype(jnp.int32) for g in range(1, block // cap))
    first = row + cap * group
    return [jnp.where(column == first + k * cap, 1.0, 0.0).astype(BF16) for k in (0, 1)]


def unpack_one_body(cap, raw_ref, out_ref):
    width = raw_ref.shape[1]
    picks = unpack_picks(out_ref.shape[0], cap)
    raw = raw_ref[...]
    for k in (0, 1):
        out_ref[:, k * width : (k + 1) * width] = jnp.dot(
            picks[k], raw, preferred_element_type=F32
        ).astype(BF16)


def unpack_one(raw, cap):
    rows, width = raw.shape[0] // 2, raw.shape[1]
    block = 160
    return kernel_call(
        functools.partial(unpack_one_body, cap),
        "unpack_one",
        grid=(rows // block,),
        in_specs=[pl.BlockSpec((2 * block, width), lambda i: (i, 0))],
        out_specs=pl.BlockSpec((block, 2 * width), lambda i: (i, 0)),
        out_shape=jax.ShapeDtypeStruct((rows, 2 * width), BF16),
    )(raw)


def add_half_body(start, rows_ref, half_ref, out_ref):
    width = half_ref.shape[1]
    out_ref[...] = rows_ref[...]
    side = (slice(None), slice(start, start + width))
    out_ref[side] = (rows_ref[side].astype(F32) + half_ref[...].astype(F32)).astype(BF16)


def add_half(rows, half, start):
    return kernel_call(
        functools.partial(add_half_body, start),
        "add_half",
        out_shape=jax.ShapeDtypeStruct(rows.shape, BF16),
        cost_estimate=FREE,
    )(rows, half)


def sum_three(refs):
    return sum(ref[...].astype(F32) for ref in refs)


def hidden_body(own_ref, below_ref, above_ref, hidden_ref, sums_ref):
    sums = sum_three((own_ref, below_ref, above_ref))
    sums_ref[...] = sums
    hidden_ref[...] = activate(sums[:, :SLOTS], sums[:, SLOTS:])


def hidden_of(parts):
    rows, n = parts[0].shape
    return kernel_call(
        hidden_body,
        "hidden",
        out_shape=[
            jax.ShapeDtypeStruct((rows, n // 2), BF16),
            jax.ShapeDtypeStruct((rows, n), F32),
        ],
        cost_estimate=FREE,
    )(*parts)


def backprop_body(own_ref, below_ref, above_ref, sums_ref, out_ref):
    back = sum_three((own_ref, below_ref, above_ref))
    d_gate, d_up = backprop(back, sums_ref[:, :SLOTS], sums_ref[:, SLOTS:])
    out_ref[:, :SLOTS] = d_gate
    out_ref[:, SLOTS:] = d_up


def backprop_of(parts, sums):
    return kernel_call(
        backprop_body,
        "backprop",
        out_shape=jax.ShapeDtypeStruct(sums.shape, BF16),
        cost_estimate=FREE,
    )(*parts, sums)


def interleave_body(core_ref, own_ref, other_ref, out_ref):
    core = core_ref[0]
    out_ref[:, core] = own_ref[...]
    out_ref[:, 1 - core] = other_ref[...]


def interleave(own, other, core):
    ys, rows, n = own.shape
    return kernel_call(
        interleave_body,
        "interleave",
        in_specs=[
            pl.BlockSpec(memory_space=pltpu.SMEM),
            pl.BlockSpec(memory_space=pltpu.VMEM),
            pl.BlockSpec(memory_space=pltpu.VMEM),
        ],
        out_shape=jax.ShapeDtypeStruct((ys, 2, rows, n), own.dtype),
        cost_estimate=FREE,
    )(core[None], own, other)


def pair_body(core_ref, value_ref, other_ref, out_ref):
    own = value_ref[:, core_ref[0]]
    out_ref[...] = (own.astype(F32) + other_ref[...].astype(F32)).astype(BF16)


def pair_sum(core, value, other):
    vmem = pl.BlockSpec(memory_space=pltpu.VMEM)
    return kernel_call(
        pair_body,
        "pair_sum",
        in_specs=[pl.BlockSpec(memory_space=pltpu.SMEM), vmem, vmem],
        out_shape=jax.ShapeDtypeStruct(other.shape, BF16),
        cost_estimate=FREE,
    )(core[None], value, other)


def column_body(y_ref, own_ref, below_ref, above_ref, low_ref, high_ref, out_ref):
    ys, half = out_ref.shape[0], low_ref.shape[1]
    y = y_ref[0]
    out_ref[y] = own_ref[...]
    out_ref[lax.rem(y + ys - 1, ys)] = below_ref[...]
    out_ref[lax.rem(y + 1, ys)] = above_ref[...]
    far = lax.rem(y + 2, ys)
    out_ref[far, :, :half] = low_ref[...]
    out_ref[far, :, half:] = high_ref[...]


def column(y, own, below, above, low, high):
    ys = lax.axis_size("y")
    vmem = pl.BlockSpec(memory_space=pltpu.VMEM)
    return kernel_call(
        column_body,
        "column",
        in_specs=[pl.BlockSpec(memory_space=pltpu.SMEM)] + [vmem] * 5,
        out_shape=jax.ShapeDtypeStruct((ys,) + own.shape, own.dtype),
        cost_estimate=FREE,
    )(y[None], own, below, above, low, high)


def product_body(dims, a_ref, b_ref, out_ref):
    out_ref[...] = lax.dot_general(
        a_ref[...], b_ref[...], dims, preferred_element_type=F32
    ).astype(BF16)


def product(a, b, transposed):
    rows, depth = a.shape
    n = b.shape[0 if transposed else 1]
    block = 256
    dims = (((1,), (1 if transposed else 0,)), ((), ()))
    return kernel_call(
        functools.partial(product_body, dims),
        "product",
        grid=(rows // block,),
        in_specs=[
            pl.BlockSpec((block, depth), lambda i: (i, 0)),
            pl.BlockSpec(b.shape, lambda i: (0, 0)),
        ],
        out_specs=pl.BlockSpec((block, n), lambda i: (i, 0)),
        out_shape=jax.ShapeDtypeStruct((rows, n), BF16),
        cost_estimate=FREE,
    )(a, b)


def column_of(row):
    n = row.shape[1]
    same = iota((n, n), 0) == iota((n, n), 1)
    return jnp.sum(jnp.where(same, row, jnp.zeros_like(row)), axis=1, keepdims=True)


def combine_body(scaled, experts, cap, *refs):
    route_ref, rows_ref, out_ref = refs[0], refs[-2], refs[-1]
    count, total = out_ref.shape[0], rows_ref.shape[0]
    places = [column_of(place) for place in token_places(route_ref, experts, cap)]
    slot = iota((count, total), 1)
    hits = [slot == place for place in places]
    rows = rows_ref[...]
    if scaled:
        shares = [column_of(share) for share in token_shares(refs[1])]
        weight = jnp.where(hits[0], shares[0], 0.0) + jnp.where(hits[1], shares[1], 0.0)
        high = weight.astype(BF16)
        low = (weight - high.astype(F32)).astype(BF16)
        total_rows = jnp.dot(high, rows, preferred_element_type=F32) + jnp.dot(
            low, rows, preferred_element_type=F32
        )
    else:
        pick = jnp.where(hits[0] | hits[1], 1.0, 0.0).astype(BF16)
        total_rows = jnp.dot(pick, rows, preferred_element_type=F32)
    out_ref[...] = total_rows.astype(BF16)


def combine(route, score, rows, experts, cap, scaled):
    count = route.shape[1]
    total, width = rows.shape
    block = 512
    whole = lambda i: (0, 0)
    return kernel_call(
        functools.partial(combine_body, scaled, experts, cap),
        "combine",
        grid=(width // block,),
        in_specs=[pl.BlockSpec((2, count), whole)] * (2 if scaled else 1)
        + [pl.BlockSpec((total, block), lambda i: (0, i))],
        out_specs=pl.BlockSpec((count, block), lambda i: (0, i)),
        out_shape=jax.ShapeDtypeStruct((count, width), BF16),
    )(*((route, score) if scaled else (route,)), rows)


def exchange(rows, parts):
    total, width = rows.shape
    return lax.all_to_all(
        rows.reshape(parts, total // parts, width),
        EXPERT,
        split_axis=0,
        concat_axis=0,
        tiled=True,
    ).reshape(total, width)


def after(value, other):
    return lax.optimization_barrier((value, other))[0]


def shift(value, axis, step):
    size = lax.axis_size(axis)
    return lax.ppermute(value, axis, [(i, (i + step) % size) for i in range(size)])


def pick(value, index, axis):
    return lax.dynamic_index_in_dim(value, index, axis, keepdims=False)


def put(value, part, y, core):
    return lax.dynamic_update_slice(value, part[None, None], (y, core, 0, 0))


def scatter_sum(value):
    rows, n = value.shape
    ys, cores = lax.axis_size("y"), lax.axis_size("core")
    y, core = lax.axis_index("y"), lax.axis_index("core")
    value = value.reshape(ys, cores, rows // (ys * cores), n)
    other = shift(pick(value, 1 - core, 1), "core", 1)
    pair = pair_sum(core, value, other)
    half = n // 256 * 128
    far = pick(pair, (y + 2) % ys, 0)
    low = shift(far[:, :half], "y", 1)
    high = shift(far[:, half:], "y", -1)
    to_above = add_half(pick(pair, (y + 1) % ys, 0), low, 0)
    to_below = add_half(pick(pair, (y + ys - 1) % ys, 0), high, half)
    return pick(pair, y, 0), shift(to_above, "y", 1), shift(to_below, "y", -1)


def gather_blocks(part):
    rows, n = part.shape
    ys, cores = lax.axis_size("y"), lax.axis_size("core")
    y, core = lax.axis_index("y"), lax.axis_index("core")
    half = n // 256 * 128
    from_below = shift(part, "y", 1)
    from_above = shift(part, "y", -1)
    low = shift(from_below[:, :half], "y", 1)
    high = shift(from_above[:, half:], "y", -1)
    held = column(y, part, from_below, from_above, low, high)
    other = shift(held, "core", 1)
    return interleave(held, other, core).reshape(ys * cores * rows, n)


def activate(gate, upper):
    sig = jax.nn.sigmoid(gate)
    return (gate * sig * upper).astype(BF16)


def backprop(back, gate, upper):
    sig = jax.nn.sigmoid(gate)
    d_gate = (back * upper * sig * (1.0 + gate * (1.0 - sig))).astype(BF16)
    d_up = (back * gate * sig).astype(BF16)
    return d_gate, d_up


def body(tokens, cotangent, route, score, clusters, w_gate, w_up, w_down):
    experts = lax.axis_size(EXPERT)
    pair_cap = SLOTS // experts
    tok_count, width = tokens.shape
    tok_cap = 4 * tok_count // experts
    route, score, ids = route.T, score.T, clusters.T
    over_rows = (((0,), (0,)), ((), ()))

    sent = load(route, ids, tokens, w_gate, w_up, experts, tok_cap, pair_cap)
    raw = lax.all_to_all(sent, EXPERT, split_axis=0, concat_axis=0, tiled=True)
    packed_down = pack(ids, w_down, w_down, experts, pair_cap, width // 2, (0, 1))
    raw_down = exchange(after(packed_down, raw), experts)
    rows_x, gate_up_rows = unload(raw, tok_cap, pair_cap)
    part = product(rows_x, gate_up_rows, True)
    sent_grads = dispatch(route, score, cotangent, experts, tok_cap, True)
    rows_dy = exchange(after(sent_grads, (raw_down, part)), experts)
    hidden, sums = hidden_of(scatter_sum(part))
    hidden = gather_blocks(hidden)
    down_rows = unpack_one(raw_down, pair_cap)
    out_part = product(hidden, down_rows, False)
    out_part, rows_dy = lax.optimization_barrier((out_part, rows_dy))
    back_out = exchange(out_part, experts)

    back = scatter_sum(product(rows_dy, down_rows, True))
    d_both = gather_blocks(backprop_of(back, sums))
    input_part = product(d_both, gate_up_rows, False)
    back_in = exchange(after(input_part, back_out), experts)

    d_both, hidden, rows_dy = after((d_both, hidden, rows_dy), input_part)
    grad_down = lax.dot_general(hidden, rows_dy, over_rows, preferred_element_type=F32)
    grad_gate = lax.dot_general(
        d_both[:, :SLOTS], rows_x, over_rows, preferred_element_type=F32
    )
    grad_up = lax.dot_general(d_both[:, SLOTS:], rows_x, over_rows, preferred_element_type=F32)
    mixed = combine(route, score, back_out, experts, tok_cap, True)
    input_grad = combine(route, score, back_in, experts, tok_cap, False)
    return (
        mixed,
        input_grad,
        grad_gate.astype(BF16)[None],
        grad_up.astype(BF16)[None],
        grad_down.astype(BF16)[None],
    )


def solution(mesh):
    fine = Mesh(mesh.devices.reshape(4, 2, 8, 4), DP + EXPERT)
    full, rows_only = P(EXPERT, DP), P(EXPERT, None)
    grads = P(EXPERT, None, DP)
    return jax.shard_map(
        body,
        mesh=fine,
        in_specs=(full, full, rows_only, rows_only, rows_only, full, full, full),
        out_specs=(full, full, grads, grads, grads),
        check_vma=False,
    )
```

```python
import functools

import jax
import jax.numpy as jnp
from jax import lax
from jax.experimental import pallas as pl
from jax.experimental.pallas import tpu as pltpu
from jax.sharding import Mesh
from jax.sharding import PartitionSpec as P

SLOTS = 640
EXPERT = ("z", "x")
DP = ("y", "core")
BF16 = jnp.bfloat16
F32 = jnp.float32
LIMIT = 48 * 1024 * 1024
FREE = pl.CostEstimate(flops=0, bytes_accessed=0, transcendentals=0)


def iota(shape, axis):
    return lax.broadcasted_iota(jnp.int32, shape, axis)


def kernel_call(body, name, **kwargs):
    return pl.pallas_call(
        body,
        name=name,
        compiler_params=pltpu.CompilerParams(vmem_limit_bytes=LIMIT),
        **kwargs,
    )


def ranks(rows, count):
    n = rows[0].shape[1]
    hits = [iota((count, n), 0) == ids for ids in rows]
    seen = sum(hit.astype(F32) for hit in hits).astype(BF16)
    earlier = (iota((n, n), 0) < iota((n, n), 1)).astype(F32).astype(BF16)
    before = jnp.dot(seen, earlier, preferred_element_type=F32)
    return [
        jnp.sum(jnp.where(hit, before, 0.0), axis=0, keepdims=True).astype(jnp.int32)
        for hit in hits
    ]


def token_places(route_ref, experts, cap):
    rows = [route_ref[0:1, :], route_ref[1:2, :]]
    return [ids * cap + rank for ids, rank in zip(rows, ranks(rows, experts))]


def token_shares(score_ref):
    score = score_ref[...].astype(F32)
    first, second = score[0:1, :], score[1:2, :]
    total = first + second
    return first / total, second / total


def dispatch_body(scaled, experts, cap, *refs):
    route_ref, x_ref, out_ref = refs[0], refs[-2], refs[-1]
    block, count = out_ref.shape[0], x_ref.shape[0]
    places = token_places(route_ref, experts, cap)
    slot = iota((block, count), 0) + pl.program_id(0) * block
    hits = [slot == place for place in places]
    pick = jnp.where(hits[0] | hits[1], 1.0, 0.0).astype(BF16)
    rows = jnp.dot(pick, x_ref[...], preferred_element_type=F32)
    if scaled:
        shares = token_shares(refs[1])
        weight = jnp.where(hits[0], shares[0], 0.0) + jnp.where(hits[1], shares[1], 0.0)
        rows = rows * jnp.sum(weight, axis=1, keepdims=True)
    out_ref[...] = rows.astype(BF16)


def dispatch(route, score, x, experts, cap, scaled):
    count, width = x.shape
    block = 256
    total = experts * cap
    whole = lambda i: (0, 0)
    return kernel_call(
        functools.partial(dispatch_body, scaled, experts, cap),
        "dispatch",
        grid=(total // block,),
        in_specs=[pl.BlockSpec((2, count), whole)] * (2 if scaled else 1)
        + [pl.BlockSpec((count, width), whole)],
        out_specs=pl.BlockSpec((block, width), lambda i: (i, 0)),
        out_shape=jax.ShapeDtypeStruct((total, width), BF16),
    )(*((route, score) if scaled else (route,)), x)


def pack_body(experts, cap, ids_ref, a_ref, b_ref, out_ref):
    block, count = out_ref.shape[0], a_ref.shape[0]
    ids = ids_ref[...]
    place = ids * (2 * cap) + ranks([ids], experts)[0]
    slot = iota((block, count), 0) + pl.program_id(0) * block
    pick_a = jnp.where(slot == place, 1.0, 0.0).astype(BF16)
    pick_b = jnp.where(slot == place + cap, 1.0, 0.0).astype(BF16)
    out_ref[...] = (
        jnp.dot(pick_a, a_ref[...], preferred_element_type=F32)
        + jnp.dot(pick_b, b_ref[...], preferred_element_type=F32)
    ).astype(BF16)


def pack(ids, a, b, experts, cap, width, columns):
    count = a.shape[0]
    block = 256
    total = 2 * experts * cap
    whole = lambda i: (0, 0)
    return kernel_call(
        functools.partial(pack_body, experts, cap),
        "pack",
        grid=(total // block,),
        in_specs=[
            pl.BlockSpec((1, count), whole),
            pl.BlockSpec((count, width), lambda i: (0, columns[0])),
            pl.BlockSpec((count, width), lambda i: (0, columns[1])),
        ],
        out_specs=pl.BlockSpec((block, width), lambda i: (i, 0)),
        out_shape=jax.ShapeDtypeStruct((total, width), BF16),
    )(ids, a, b)


def load_body(
    experts, cap, pair_cap, route_ref, ids_ref, x_ref, a_ref, b_ref, out_ref, token_at, row_at
):
    per = out_ref.shape[0]
    first = pl.program_id(0) * per
    pairs = 2 * pair_cap

    @pl.when(pl.program_id(0) == 0)
    def _():
        for k, place in enumerate(token_places(route_ref, experts, cap)):
            token_at[k : k + 1, :] = place
        ids = ids_ref[...]
        row_at[0:1, :] = ids * pairs + ranks([ids], experts)[0]

    places = [token_at[k : k + 1, :] for k in (0, 1)]
    slot = iota((per * cap, x_ref.shape[0]), 0) + first * cap
    pick = jnp.where((slot == places[0]) | (slot == places[1]), 1.0, 0.0).astype(BF16)
    tokens = jnp.dot(pick, x_ref[...], preferred_element_type=F32)
    place = row_at[0:1, :]
    slot = iota((per * pairs, a_ref.shape[0]), 0) + first * pairs
    pick_a = jnp.where(slot == place, 1.0, 0.0).astype(BF16)
    pick_b = jnp.where(slot == place + pair_cap, 1.0, 0.0).astype(BF16)
    weights = jnp.dot(pick_a, a_ref[...], preferred_element_type=F32) + jnp.dot(
        pick_b, b_ref[...], preferred_element_type=F32
    )
    for k in range(per):
        out_ref[k, :cap, :] = tokens[k * cap : (k + 1) * cap, :].astype(BF16)
        out_ref[k, cap:, :] = weights[k * pairs : (k + 1) * pairs, :].astype(BF16)


def load(route, ids, x, a, b, experts, cap, pair_cap):
    width = x.shape[1]
    per = 4
    whole = lambda i: (0, 0)
    return kernel_call(
        functools.partial(load_body, experts, cap, pair_cap),
        "load",
        grid=(experts // per,),
        in_specs=[pl.BlockSpec(v.shape, whole) for v in (route, ids, x, a, b)],
        out_specs=pl.BlockSpec((per, cap + 2 * pair_cap, width), lambda i: (i, 0, 0)),
        out_shape=jax.ShapeDtypeStruct((experts, cap + 2 * pair_cap, width), BF16),
        scratch_shapes=[
            pltpu.VMEM((8, x.shape[0]), jnp.int32),
            pltpu.VMEM((8, a.shape[0]), jnp.int32),
        ],
    )(route, ids, x, a, b)


def unload_body(cap, pair_cap, raw_ref, rows_ref, weights_ref):
    per = raw_ref.shape[0]
    for k in range(per):
        rows_ref[k * cap : (k + 1) * cap, :] = raw_ref[k, :cap, :]
    raw = jnp.concatenate(
        [raw_ref[k, cap:, :].astype(F32) for k in range(per)], axis=0
    ).astype(BF16)
    picks = unpack_picks(weights_ref.shape[1], pair_cap)
    for k in (0, 1):
        weights_ref[k] = jnp.dot(picks[k], raw, preferred_element_type=F32).astype(BF16)


def unload(raw, cap, pair_cap):
    experts, width = raw.shape[0], raw.shape[2]
    per = 8
    rows, weights = kernel_call(
        functools.partial(unload_body, cap, pair_cap),
        "unload",
        grid=(experts // per,),
        in_specs=[pl.BlockSpec((per,) + raw.shape[1:], lambda i: (i, 0, 0))],
        out_specs=[
            pl.BlockSpec((per * cap, width), lambda i: (i, 0)),
            pl.BlockSpec((2, per * pair_cap, width), lambda i: (0, i, 0)),
        ],
        out_shape=[
            jax.ShapeDtypeStruct((experts * cap, width), BF16),
            jax.ShapeDtypeStruct((2, experts * pair_cap, width), BF16),
        ],
    )(raw)
    return rows, weights.reshape(2 * experts * pair_cap, width)


def unpack_picks(block, cap):
    row, column = iota((block, 2 * block), 0), iota((block, 2 * block), 1)
    group = sum((row >= g * cap).astype(jnp.int32) for g in range(1, block // cap))
    first = row + cap * group
    return [jnp.where(column == first + k * cap, 1.0, 0.0).astype(BF16) for k in (0, 1)]


def unpack_one_body(cap, raw_ref, out_ref):
    width = raw_ref.shape[1]
    picks = unpack_picks(out_ref.shape[0], cap)
    raw = raw_ref[...]
    for k in (0, 1):
        out_ref[:, k * width : (k + 1) * width] = jnp.dot(
            picks[k], raw, preferred_element_type=F32
        ).astype(BF16)


def unpack_one(raw, cap):
    rows, width = raw.shape[0] // 2, raw.shape[1]
    block = 160
    return kernel_call(
        functools.partial(unpack_one_body, cap),
        "unpack_one",
        grid=(rows // block,),
        in_specs=[pl.BlockSpec((2 * block, width), lambda i: (i, 0))],
        out_specs=pl.BlockSpec((block, 2 * width), lambda i: (i, 0)),
        out_shape=jax.ShapeDtypeStruct((rows, 2 * width), BF16),
    )(raw)


def add_half_body(start, rows_ref, half_ref, out_ref):
    width = half_ref.shape[1]
    out_ref[...] = rows_ref[...]
    side = (slice(None), slice(start, start + width))
    out_ref[side] = (rows_ref[side].astype(F32) + half_ref[...].astype(F32)).astype(BF16)


def add_half(rows, half, start):
    return kernel_call(
        functools.partial(add_half_body, start),
        "add_half",
        out_shape=jax.ShapeDtypeStruct(rows.shape, BF16),
        cost_estimate=FREE,
    )(rows, half)


def sum_three(refs):
    return sum(ref[...].astype(F32) for ref in refs)


def hidden_body(own_ref, below_ref, above_ref, hidden_ref, sums_ref):
    sums = sum_three((own_ref, below_ref, above_ref))
    sums_ref[...] = sums
    hidden_ref[...] = activate(sums[:, :SLOTS], sums[:, SLOTS:])


def hidden_of(parts):
    rows, n = parts[0].shape
    return kernel_call(
        hidden_body,
        "hidden",
        out_shape=[
            jax.ShapeDtypeStruct((rows, n // 2), BF16),
            jax.ShapeDtypeStruct((rows, n), F32),
        ],
        cost_estimate=FREE,
    )(*parts)


def backprop_body(own_ref, below_ref, above_ref, sums_ref, out_ref):
    back = sum_three((own_ref, below_ref, above_ref))
    d_gate, d_up = backprop(back, sums_ref[:, :SLOTS], sums_ref[:, SLOTS:])
    out_ref[:, :SLOTS] = d_gate
    out_ref[:, SLOTS:] = d_up


def backprop_of(parts, sums):
    return kernel_call(
        backprop_body,
        "backprop",
        out_shape=jax.ShapeDtypeStruct(sums.shape, BF16),
        cost_estimate=FREE,
    )(*parts, sums)


def interleave_body(core_ref, own_ref, other_ref, out_ref):
    core = core_ref[0]
    out_ref[:, core] = own_ref[...]
    out_ref[:, 1 - core] = other_ref[...]


def interleave(own, other, core):
    ys, rows, n = own.shape
    return kernel_call(
        interleave_body,
        "interleave",
        in_specs=[
            pl.BlockSpec(memory_space=pltpu.SMEM),
            pl.BlockSpec(memory_space=pltpu.VMEM),
            pl.BlockSpec(memory_space=pltpu.VMEM),
        ],
        out_shape=jax.ShapeDtypeStruct((ys, 2, rows, n), own.dtype),
        cost_estimate=FREE,
    )(core[None], own, other)


def pair_body(core_ref, value_ref, other_ref, out_ref):
    own = value_ref[:, core_ref[0]]
    out_ref[...] = (own.astype(F32) + other_ref[...].astype(F32)).astype(BF16)


def pair_sum(core, value, other):
    vmem = pl.BlockSpec(memory_space=pltpu.VMEM)
    return kernel_call(
        pair_body,
        "pair_sum",
        in_specs=[pl.BlockSpec(memory_space=pltpu.SMEM), vmem, vmem],
        out_shape=jax.ShapeDtypeStruct(other.shape, BF16),
        cost_estimate=FREE,
    )(core[None], value, other)


def column_body(y_ref, own_ref, below_ref, above_ref, low_ref, high_ref, out_ref):
    ys, half = out_ref.shape[0], low_ref.shape[1]
    y = y_ref[0]
    out_ref[y] = own_ref[...]
    out_ref[lax.rem(y + ys - 1, ys)] = below_ref[...]
    out_ref[lax.rem(y + 1, ys)] = above_ref[...]
    far = lax.rem(y + 2, ys)
    out_ref[far, :, :half] = low_ref[...]
    out_ref[far, :, half:] = high_ref[...]


def column(y, own, below, above, low, high):
    ys = lax.axis_size("y")
    vmem = pl.BlockSpec(memory_space=pltpu.VMEM)
    return kernel_call(
        column_body,
        "column",
        in_specs=[pl.BlockSpec(memory_space=pltpu.SMEM)] + [vmem] * 5,
        out_shape=jax.ShapeDtypeStruct((ys,) + own.shape, own.dtype),
        cost_estimate=FREE,
    )(y[None], own, below, above, low, high)


def product_body(dims, a_ref, b_ref, out_ref):
    out_ref[...] = lax.dot_general(
        a_ref[...], b_ref[...], dims, preferred_element_type=F32
    ).astype(BF16)


def product(a, b, transposed):
    rows, depth = a.shape
    n = b.shape[0 if transposed else 1]
    block = 256
    dims = (((1,), (1 if transposed else 0,)), ((), ()))
    return kernel_call(
        functools.partial(product_body, dims),
        "product",
        grid=(rows // block,),
        in_specs=[
            pl.BlockSpec((block, depth), lambda i: (i, 0)),
            pl.BlockSpec(b.shape, lambda i: (0, 0)),
        ],
        out_specs=pl.BlockSpec((block, n), lambda i: (i, 0)),
        out_shape=jax.ShapeDtypeStruct((rows, n), BF16),
        cost_estimate=FREE,
    )(a, b)


def column_of(row):
    n = row.shape[1]
    same = iota((n, n), 0) == iota((n, n), 1)
    return jnp.sum(jnp.where(same, row, jnp.zeros_like(row)), axis=1, keepdims=True)


def combine_body(scaled, experts, cap, *refs):
    terms = 2 if scaled else 1
    route_ref, rows_ref, out_ref = refs[0], refs[terms], refs[terms + 1]
    picks = refs[terms + 2 :]
    count, total = out_ref.shape[0], rows_ref.shape[0]

    @pl.when(pl.program_id(0) == 0)
    def _():
        places = [column_of(place) for place in token_places(route_ref, experts, cap)]
        slot = iota((count, total), 1)
        hits = [slot == place for place in places]
        if scaled:
            shares = [column_of(share) for share in token_shares(refs[1])]
            weight = jnp.where(hits[0], shares[0], 0.0) + jnp.where(hits[1], shares[1], 0.0)
            high = weight.astype(BF16)
            picks[0][...] = high
            picks[1][...] = (weight - high.astype(F32)).astype(BF16)
        else:
            picks[0][...] = jnp.where(hits[0] | hits[1], 1.0, 0.0).astype(BF16)

    rows = rows_ref[...]
    out_ref[...] = sum(
        jnp.dot(pick[...], rows, preferred_element_type=F32) for pick in picks
    ).astype(BF16)


def combine(route, score, rows, experts, cap, scaled):
    count = route.shape[1]
    total, width = rows.shape
    block = 256
    whole = lambda i: (0, 0)
    terms = 2 if scaled else 1
    return kernel_call(
        functools.partial(combine_body, scaled, experts, cap),
        "combine",
        grid=(width // block,),
        in_specs=[pl.BlockSpec((2, count), whole)] * terms
        + [pl.BlockSpec((total, block), lambda i: (0, i))],
        out_specs=pl.BlockSpec((count, block), lambda i: (0, i)),
        out_shape=jax.ShapeDtypeStruct((count, width), BF16),
        scratch_shapes=[pltpu.VMEM((count, total), BF16)] * terms,
    )(*((route, score) if scaled else (route,)), rows)


def exchange(rows, parts):
    total, width = rows.shape
    return lax.all_to_all(
        rows.reshape(parts, total // parts, width),
        EXPERT,
        split_axis=0,
        concat_axis=0,
        tiled=True,
    ).reshape(total, width)


def after(value, other):
    return lax.optimization_barrier((value, other))[0]


def shift(value, axis, step):
    size = lax.axis_size(axis)
    return lax.ppermute(value, axis, [(i, (i + step) % size) for i in range(size)])


def pick(value, index, axis):
    return lax.dynamic_index_in_dim(value, index, axis, keepdims=False)


def put(value, part, y, core):
    return lax.dynamic_update_slice(value, part[None, None], (y, core, 0, 0))


def scatter_start(value):
    rows, n = value.shape
    ys, cores = lax.axis_size("y"), lax.axis_size("core")
    y, core = lax.axis_index("y"), lax.axis_index("core")
    value = value.reshape(ys, cores, rows // (ys * cores), n)
    other = shift(pick(value, 1 - core, 1), "core", 1)
    pair = pair_sum(core, value, other)
    half = n // 256 * 128
    far = pick(pair, (y + 2) % ys, 0)
    low = shift(far[:, :half], "y", 1)
    high = shift(far[:, half:], "y", -1)
    to_above = add_half(pick(pair, (y + 1) % ys, 0), low, 0)
    to_below = add_half(pick(pair, (y + ys - 1) % ys, 0), high, half)
    return pick(pair, y, 0), to_above, to_below


def scatter_end(own, to_above, to_below):
    return own, shift(to_above, "y", 1), shift(to_below, "y", -1)


def gather_blocks(part):
    rows, n = part.shape
    ys, cores = lax.axis_size("y"), lax.axis_size("core")
    y, core = lax.axis_index("y"), lax.axis_index("core")
    half = n // 256 * 128
    from_below = shift(part, "y", 1)
    from_above = shift(part, "y", -1)
    low = shift(from_below[:, :half], "y", 1)
    high = shift(from_above[:, half:], "y", -1)
    held = column(y, part, from_below, from_above, low, high)
    other = shift(held, "core", 1)
    return interleave(held, other, core).reshape(ys * cores * rows, n)


def activate(gate, upper):
    sig = jax.nn.sigmoid(gate)
    return (gate * sig * upper).astype(BF16)


def backprop(back, gate, upper):
    sig = jax.nn.sigmoid(gate)
    d_gate = (back * upper * sig * (1.0 + gate * (1.0 - sig))).astype(BF16)
    d_up = (back * gate * sig).astype(BF16)
    return d_gate, d_up


def body(tokens, cotangent, route, score, clusters, w_gate, w_up, w_down):
    experts = lax.axis_size(EXPERT)
    pair_cap = SLOTS // experts
    tok_count, width = tokens.shape
    tok_cap = 4 * tok_count // experts
    route, score, ids = route.T, score.T, clusters.T
    over_rows = (((0,), (0,)), ((), ()))

    sent = load(route, ids, tokens, w_gate, w_up, experts, tok_cap, pair_cap)
    raw = lax.all_to_all(sent, EXPERT, split_axis=0, concat_axis=0, tiled=True)
    packed_down = pack(ids, w_down, w_down, experts, pair_cap, width // 2, (0, 1))
    sent_grads = dispatch(route, score, cotangent, experts, tok_cap, True)
    raw_down = exchange(after(packed_down, (raw, sent_grads)), experts)
    rows_x, gate_up_rows = unload(raw, tok_cap, pair_cap)
    steps = scatter_start(product(rows_x, gate_up_rows, True))
    rows_dy = exchange(after(sent_grads, (raw_down, steps)), experts)
    terms = scatter_end(*steps)
    hidden, sums = hidden_of(terms)
    hidden = gather_blocks(hidden)
    down_rows = unpack_one(raw_down, pair_cap)
    out_part = product(hidden, down_rows, False)
    out_part, rows_dy = lax.optimization_barrier((out_part, rows_dy))
    back_out = exchange(out_part, experts)

    back = scatter_end(*scatter_start(product(rows_dy, down_rows, True)))
    d_both = gather_blocks(backprop_of(back, sums))
    input_part = product(d_both, gate_up_rows, False)
    back_in = exchange(after(input_part, back_out), experts)

    d_both, hidden, rows_dy = after((d_both, hidden, rows_dy), input_part)
    grad_down = lax.dot_general(hidden, rows_dy, over_rows, preferred_element_type=F32)
    grad_gate = lax.dot_general(
        d_both[:, :SLOTS], rows_x, over_rows, preferred_element_type=F32
    )
    grad_up = lax.dot_general(d_both[:, SLOTS:], rows_x, over_rows, preferred_element_type=F32)
    mixed = combine(route, score, back_out, experts, tok_cap, True)
    input_grad = combine(route, score, back_in, experts, tok_cap, False)
    return (
        mixed,
        input_grad,
        grad_gate.astype(BF16)[None],
        grad_up.astype(BF16)[None],
        grad_down.astype(BF16)[None],
    )


def solution(mesh):
    fine = Mesh(mesh.devices.reshape(4, 2, 8, 4), DP + EXPERT)
    full, rows_only = P(EXPERT, DP), P(EXPERT, None)
    grads = P(EXPERT, None, DP)
    return jax.shard_map(
        body,
        mesh=fine,
        in_specs=(full, full, rows_only, rows_only, rows_only, full, full, full),
        out_specs=(full, full, grads, grads, grads),
        check_vma=False,
    )
```

```python
import functools

import jax
import jax.numpy as jnp
from jax import lax
from jax.experimental import pallas as pl
from jax.experimental.pallas import tpu as pltpu
from jax.sharding import Mesh
from jax.sharding import PartitionSpec as P

SLOTS = 640
EXPERT = ("z", "x")
DP = ("y", "core")
BF16 = jnp.bfloat16
F32 = jnp.float32
LIMIT = 48 * 1024 * 1024
MOST = 63 * 1024 * 1024
FREE = pl.CostEstimate(flops=0, bytes_accessed=0, transcendentals=0)


def iota(shape, axis):
    return lax.broadcasted_iota(jnp.int32, shape, axis)


def kernel_call(body, name, limit=LIMIT, **kwargs):
    return pl.pallas_call(
        body,
        name=name,
        compiler_params=pltpu.CompilerParams(vmem_limit_bytes=limit),
        **kwargs,
    )


def ranks(rows, count):
    n = rows[0].shape[1]
    hits = [iota((count, n), 0) == ids for ids in rows]
    seen = sum(hit.astype(F32) for hit in hits).astype(BF16)
    earlier = (iota((n, n), 0) < iota((n, n), 1)).astype(F32).astype(BF16)
    before = jnp.dot(seen, earlier, preferred_element_type=F32)
    return [
        jnp.sum(jnp.where(hit, before, 0.0), axis=0, keepdims=True).astype(jnp.int32)
        for hit in hits
    ]


def token_places(route_ref, experts, cap):
    rows = [route_ref[0:1, :], route_ref[1:2, :]]
    return [ids * cap + rank for ids, rank in zip(rows, ranks(rows, experts))]


def token_shares(score_ref):
    score = score_ref[...].astype(F32)
    first, second = score[0:1, :], score[1:2, :]
    total = first + second
    return first / total, second / total


def dispatch_body(scaled, experts, cap, *refs):
    route_ref, x_ref, out_ref = refs[0], refs[-2], refs[-1]
    block, count = out_ref.shape[0], x_ref.shape[0]
    places = token_places(route_ref, experts, cap)
    slot = iota((block, count), 0) + pl.program_id(0) * block
    hits = [slot == place for place in places]
    pick = jnp.where(hits[0] | hits[1], 1.0, 0.0).astype(BF16)
    rows = jnp.dot(pick, x_ref[...], preferred_element_type=F32)
    if scaled:
        shares = token_shares(refs[1])
        weight = jnp.where(hits[0], shares[0], 0.0) + jnp.where(hits[1], shares[1], 0.0)
        rows = rows * jnp.sum(weight, axis=1, keepdims=True)
    out_ref[...] = rows.astype(BF16)


def dispatch(route, score, x, experts, cap, scaled):
    count, width = x.shape
    block = 256
    total = experts * cap
    whole = lambda i: (0, 0)
    return kernel_call(
        functools.partial(dispatch_body, scaled, experts, cap),
        "dispatch",
        grid=(total // block,),
        in_specs=[pl.BlockSpec((2, count), whole)] * (2 if scaled else 1)
        + [pl.BlockSpec((count, width), whole)],
        out_specs=pl.BlockSpec((block, width), lambda i: (i, 0)),
        out_shape=jax.ShapeDtypeStruct((total, width), BF16),
    )(*((route, score) if scaled else (route,)), x)


def pack_body(experts, cap, ids_ref, a_ref, b_ref, out_ref):
    block, count = out_ref.shape[0], a_ref.shape[0]
    ids = ids_ref[...]
    place = ids * (2 * cap) + ranks([ids], experts)[0]
    slot = iota((block, count), 0) + pl.program_id(0) * block
    pick_a = jnp.where(slot == place, 1.0, 0.0).astype(BF16)
    pick_b = jnp.where(slot == place + cap, 1.0, 0.0).astype(BF16)
    out_ref[...] = (
        jnp.dot(pick_a, a_ref[...], preferred_element_type=F32)
        + jnp.dot(pick_b, b_ref[...], preferred_element_type=F32)
    ).astype(BF16)


def pack(ids, a, b, experts, cap, width, columns):
    count = a.shape[0]
    block = 256
    total = 2 * experts * cap
    whole = lambda i: (0, 0)
    return kernel_call(
        functools.partial(pack_body, experts, cap),
        "pack",
        grid=(total // block,),
        in_specs=[
            pl.BlockSpec((1, count), whole),
            pl.BlockSpec((count, width), lambda i: (0, columns[0])),
            pl.BlockSpec((count, width), lambda i: (0, columns[1])),
        ],
        out_specs=pl.BlockSpec((block, width), lambda i: (i, 0)),
        out_shape=jax.ShapeDtypeStruct((total, width), BF16),
    )(ids, a, b)


def load_body(experts, cap, pair_cap, route_ref, ids_ref, *refs):
    held_in, out_ref, token_at, row_at = refs[:3], refs[3], refs[4], refs[5]
    held, sems = refs[6:9], refs[9]
    per = out_ref.shape[0]
    first = pl.program_id(0) * per
    pairs = 2 * pair_cap

    @pl.when(pl.program_id(0) == 0)
    def _():
        copies = [
            pltpu.make_async_copy(source, target, sems.at[k])
            for k, (source, target) in enumerate(zip(held_in, held))
        ]
        for copy in copies:
            copy.start()
        for k, place in enumerate(token_places(route_ref, experts, cap)):
            token_at[k : k + 1, :] = place
        ids = ids_ref[...]
        row_at[0:1, :] = ids * pairs + ranks([ids], experts)[0]
        for copy in copies:
            copy.wait()

    x_ref, a_ref, b_ref = held
    places = [token_at[k : k + 1, :] for k in (0, 1)]
    slot = iota((per * cap, x_ref.shape[0]), 0) + first * cap
    pick = jnp.where((slot == places[0]) | (slot == places[1]), 1.0, 0.0).astype(BF16)
    tokens = jnp.dot(pick, x_ref[...], preferred_element_type=F32)
    place = row_at[0:1, :]
    slot = iota((per * pairs, a_ref.shape[0]), 0) + first * pairs
    pick_a = jnp.where(slot == place, 1.0, 0.0).astype(BF16)
    pick_b = jnp.where(slot == place + pair_cap, 1.0, 0.0).astype(BF16)
    weights = jnp.dot(pick_a, a_ref[...], preferred_element_type=F32) + jnp.dot(
        pick_b, b_ref[...], preferred_element_type=F32
    )
    for k in range(per):
        out_ref[k, :cap, :] = tokens[k * cap : (k + 1) * cap, :].astype(BF16)
        out_ref[k, cap:, :] = weights[k * pairs : (k + 1) * pairs, :].astype(BF16)


def load(route, ids, x, a, b, experts, cap, pair_cap):
    width = x.shape[1]
    per = 4
    whole = lambda i: (0, 0)
    return kernel_call(
        functools.partial(load_body, experts, cap, pair_cap),
        "load",
        MOST,
        grid=(experts // per,),
        in_specs=[pl.BlockSpec(v.shape, whole) for v in (route, ids)]
        + [pl.BlockSpec(memory_space=pltpu.HBM)] * 3,
        out_specs=pl.BlockSpec((per, cap + 2 * pair_cap, width), lambda i: (i, 0, 0)),
        out_shape=jax.ShapeDtypeStruct((experts, cap + 2 * pair_cap, width), BF16),
        scratch_shapes=[
            pltpu.VMEM((8, x.shape[0]), jnp.int32),
            pltpu.VMEM((8, a.shape[0]), jnp.int32),
        ]
        + [pltpu.VMEM(v.shape, v.dtype) for v in (x, a, b)]
        + [pltpu.SemaphoreType.DMA((3,))],
    )(route, ids, x, a, b)


def unload_body(cap, pair_cap, raw_ref, rows_ref, weights_ref):
    per = raw_ref.shape[0]
    for k in range(per):
        rows_ref[k * cap : (k + 1) * cap, :] = raw_ref[k, :cap, :]
    raw = jnp.concatenate(
        [raw_ref[k, cap:, :].astype(F32) for k in range(per)], axis=0
    ).astype(BF16)
    picks = unpack_picks(weights_ref.shape[1], pair_cap)
    for k in (0, 1):
        weights_ref[k] = jnp.dot(picks[k], raw, preferred_element_type=F32).astype(BF16)


def unload(raw, cap, pair_cap):
    experts, width = raw.shape[0], raw.shape[2]
    per = 8
    rows, weights = kernel_call(
        functools.partial(unload_body, cap, pair_cap),
        "unload",
        grid=(experts // per,),
        in_specs=[pl.BlockSpec((per,) + raw.shape[1:], lambda i: (i, 0, 0))],
        out_specs=[
            pl.BlockSpec((per * cap, width), lambda i: (i, 0)),
            pl.BlockSpec((2, per * pair_cap, width), lambda i: (0, i, 0)),
        ],
        out_shape=[
            jax.ShapeDtypeStruct((experts * cap, width), BF16),
            jax.ShapeDtypeStruct((2, experts * pair_cap, width), BF16),
        ],
    )(raw)
    return rows, weights.reshape(2 * experts * pair_cap, width)


def unpack_picks(block, cap):
    row, column = iota((block, 2 * block), 0), iota((block, 2 * block), 1)
    group = sum((row >= g * cap).astype(jnp.int32) for g in range(1, block // cap))
    first = row + cap * group
    return [jnp.where(column == first + k * cap, 1.0, 0.0).astype(BF16) for k in (0, 1)]


def unpack_one_body(cap, raw_ref, out_ref):
    width = raw_ref.shape[1]
    picks = unpack_picks(out_ref.shape[0], cap)
    raw = raw_ref[...]
    for k in (0, 1):
        out_ref[:, k * width : (k + 1) * width] = jnp.dot(
            picks[k], raw, preferred_element_type=F32
        ).astype(BF16)


def unpack_one(raw, cap):
    rows, width = raw.shape[0] // 2, raw.shape[1]
    block = 160
    return kernel_call(
        functools.partial(unpack_one_body, cap),
        "unpack_one",
        grid=(rows // block,),
        in_specs=[pl.BlockSpec((2 * block, width), lambda i: (i, 0))],
        out_specs=pl.BlockSpec((block, 2 * width), lambda i: (i, 0)),
        out_shape=jax.ShapeDtypeStruct((rows, 2 * width), BF16),
    )(raw)


def add_half_body(start, rows_ref, half_ref, out_ref):
    width = half_ref.shape[1]
    out_ref[...] = rows_ref[...]
    side = (slice(None), slice(start, start + width))
    out_ref[side] = (rows_ref[side].astype(F32) + half_ref[...].astype(F32)).astype(BF16)


def add_half(rows, half, start):
    return kernel_call(
        functools.partial(add_half_body, start),
        "add_half",
        out_shape=jax.ShapeDtypeStruct(rows.shape, BF16),
        cost_estimate=FREE,
    )(rows, half)


def sum_three(refs):
    return sum(ref[...].astype(F32) for ref in refs)


def hidden_body(own_ref, below_ref, above_ref, hidden_ref, sums_ref):
    sums = sum_three((own_ref, below_ref, above_ref))
    sums_ref[...] = sums
    hidden_ref[...] = activate(sums[:, :SLOTS], sums[:, SLOTS:])


def hidden_of(parts):
    rows, n = parts[0].shape
    return kernel_call(
        hidden_body,
        "hidden",
        out_shape=[
            jax.ShapeDtypeStruct((rows, n // 2), BF16),
            jax.ShapeDtypeStruct((rows, n), F32),
        ],
        cost_estimate=FREE,
    )(*parts)


def backprop_body(own_ref, below_ref, above_ref, sums_ref, out_ref):
    back = sum_three((own_ref, below_ref, above_ref))
    d_gate, d_up = backprop(back, sums_ref[:, :SLOTS], sums_ref[:, SLOTS:])
    out_ref[:, :SLOTS] = d_gate
    out_ref[:, SLOTS:] = d_up


def backprop_of(parts, sums):
    return kernel_call(
        backprop_body,
        "backprop",
        out_shape=jax.ShapeDtypeStruct(sums.shape, BF16),
        cost_estimate=FREE,
    )(*parts, sums)


def interleave_body(core_ref, own_ref, other_ref, out_ref):
    core = core_ref[0]
    out_ref[:, core] = own_ref[...]
    out_ref[:, 1 - core] = other_ref[...]


def interleave(own, other, core):
    ys, rows, n = own.shape
    return kernel_call(
        interleave_body,
        "interleave",
        in_specs=[
            pl.BlockSpec(memory_space=pltpu.SMEM),
            pl.BlockSpec(memory_space=pltpu.VMEM),
            pl.BlockSpec(memory_space=pltpu.VMEM),
        ],
        out_shape=jax.ShapeDtypeStruct((ys, 2, rows, n), own.dtype),
        cost_estimate=FREE,
    )(core[None], own, other)


def pair_body(core_ref, value_ref, other_ref, out_ref):
    own = value_ref[:, core_ref[0]]
    out_ref[...] = (own.astype(F32) + other_ref[...].astype(F32)).astype(BF16)


def pair_sum(core, value, other):
    vmem = pl.BlockSpec(memory_space=pltpu.VMEM)
    return kernel_call(
        pair_body,
        "pair_sum",
        in_specs=[pl.BlockSpec(memory_space=pltpu.SMEM), vmem, vmem],
        out_shape=jax.ShapeDtypeStruct(other.shape, BF16),
        cost_estimate=FREE,
    )(core[None], value, other)


def column_body(y_ref, own_ref, below_ref, above_ref, low_ref, high_ref, out_ref):
    ys, half = out_ref.shape[0], low_ref.shape[1]
    y = y_ref[0]
    out_ref[y] = own_ref[...]
    out_ref[lax.rem(y + ys - 1, ys)] = below_ref[...]
    out_ref[lax.rem(y + 1, ys)] = above_ref[...]
    far = lax.rem(y + 2, ys)
    out_ref[far, :, :half] = low_ref[...]
    out_ref[far, :, half:] = high_ref[...]


def column(y, own, below, above, low, high):
    ys = lax.axis_size("y")
    vmem = pl.BlockSpec(memory_space=pltpu.VMEM)
    return kernel_call(
        column_body,
        "column",
        in_specs=[pl.BlockSpec(memory_space=pltpu.SMEM)] + [vmem] * 5,
        out_shape=jax.ShapeDtypeStruct((ys,) + own.shape, own.dtype),
        cost_estimate=FREE,
    )(y[None], own, below, above, low, high)


def product_body(dims, a_ref, b_ref, out_ref):
    out_ref[...] = lax.dot_general(
        a_ref[...], b_ref[...], dims, preferred_element_type=F32
    ).astype(BF16)


def product(a, b, transposed):
    rows, depth = a.shape
    n = b.shape[0 if transposed else 1]
    block = 256
    dims = (((1,), (1 if transposed else 0,)), ((), ()))
    return kernel_call(
        functools.partial(product_body, dims),
        "product",
        grid=(rows // block,),
        in_specs=[
            pl.BlockSpec((block, depth), lambda i: (i, 0)),
            pl.BlockSpec(b.shape, lambda i: (0, 0)),
        ],
        out_specs=pl.BlockSpec((block, n), lambda i: (i, 0)),
        out_shape=jax.ShapeDtypeStruct((rows, n), BF16),
        cost_estimate=FREE,
    )(a, b)


def column_of(row):
    n = row.shape[1]
    same = iota((n, n), 0) == iota((n, n), 1)
    return jnp.sum(jnp.where(same, row, jnp.zeros_like(row)), axis=1, keepdims=True)


def combine_body(experts, cap, route_ref, score_ref, rows_ref, out_ref):
    count, total = out_ref.shape[0], rows_ref.shape[0]
    places = [column_of(place) for place in token_places(route_ref, experts, cap)]
    slot = iota((count, total), 1)
    hits = [slot == place for place in places]
    rows = rows_ref[...]
    shares = [column_of(share) for share in token_shares(score_ref)]
    weight = jnp.where(hits[0], shares[0], 0.0) + jnp.where(hits[1], shares[1], 0.0)
    high = weight.astype(BF16)
    low = (weight - high.astype(F32)).astype(BF16)
    out_ref[...] = (
        jnp.dot(high, rows, preferred_element_type=F32)
        + jnp.dot(low, rows, preferred_element_type=F32)
    ).astype(BF16)


def combine(route, score, rows, experts, cap):
    count = route.shape[1]
    total, width = rows.shape
    block = 512
    whole = lambda i: (0, 0)
    return kernel_call(
        functools.partial(combine_body, experts, cap),
        "combine",
        grid=(width // block,),
        in_specs=[pl.BlockSpec((2, count), whole)] * 2
        + [pl.BlockSpec((total, block), lambda i: (0, i))],
        out_specs=pl.BlockSpec((count, block), lambda i: (0, i)),
        out_shape=jax.ShapeDtypeStruct((count, width), BF16),
    )(route, score, rows)


def pairs_body(experts, cap, route_ref, out_ref):
    places = [column_of(place) for place in token_places(route_ref, experts, cap)]
    slot = iota(out_ref.shape, 1)
    out_ref[...] = jnp.where((slot == places[0]) | (slot == places[1]), 1.0, 0.0).astype(BF16)


def token_pairs(route, experts, cap):
    return kernel_call(
        functools.partial(pairs_body, experts, cap),
        "token_pairs",
        out_shape=jax.ShapeDtypeStruct((route.shape[1], experts * cap), BF16),
    )(route)


def pair_rows_body(picks_ref, rows_ref, out_ref):
    out_ref[...] = jnp.dot(
        picks_ref[...], rows_ref[...], preferred_element_type=F32
    ).astype(BF16)


def pair_rows(picks, rows):
    count, total = picks.shape
    width = rows.shape[1]
    block = 256
    return kernel_call(
        pair_rows_body,
        "pair_rows",
        grid=(width // block,),
        in_specs=[
            pl.BlockSpec((count, total), lambda i: (0, 0)),
            pl.BlockSpec((total, block), lambda i: (0, i)),
        ],
        out_specs=pl.BlockSpec((count, block), lambda i: (0, i)),
        out_shape=jax.ShapeDtypeStruct((count, width), BF16),
    )(picks, rows)


def exchange(rows, parts):
    total, width = rows.shape
    return lax.all_to_all(
        rows.reshape(parts, total // parts, width),
        EXPERT,
        split_axis=0,
        concat_axis=0,
        tiled=True,
    ).reshape(total, width)


def after(value, other):
    return lax.optimization_barrier((value, other))[0]


def shift(value, axis, step):
    size = lax.axis_size(axis)
    return lax.ppermute(value, axis, [(i, (i + step) % size) for i in range(size)])


def pick(value, index, axis):
    return lax.dynamic_index_in_dim(value, index, axis, keepdims=False)


def put(value, part, y, core):
    return lax.dynamic_update_slice(value, part[None, None], (y, core, 0, 0))


def scatter_start(value):
    rows, n = value.shape
    ys, cores = lax.axis_size("y"), lax.axis_size("core")
    y, core = lax.axis_index("y"), lax.axis_index("core")
    value = value.reshape(ys, cores, rows // (ys * cores), n)
    other = shift(pick(value, 1 - core, 1), "core", 1)
    pair = pair_sum(core, value, other)
    half = n // 256 * 128
    far = pick(pair, (y + 2) % ys, 0)
    low = shift(far[:, :half], "y", 1)
    high = shift(far[:, half:], "y", -1)
    to_above = add_half(pick(pair, (y + 1) % ys, 0), low, 0)
    to_below = add_half(pick(pair, (y + ys - 1) % ys, 0), high, half)
    return pick(pair, y, 0), to_above, to_below


def scatter_end(own, to_above, to_below):
    return own, shift(to_above, "y", 1), shift(to_below, "y", -1)


def gather_blocks(part):
    rows, n = part.shape
    ys, cores = lax.axis_size("y"), lax.axis_size("core")
    y, core = lax.axis_index("y"), lax.axis_index("core")
    half = n // 256 * 128
    from_below = shift(part, "y", 1)
    from_above = shift(part, "y", -1)
    low = shift(from_below[:, :half], "y", 1)
    high = shift(from_above[:, half:], "y", -1)
    held = column(y, part, from_below, from_above, low, high)
    other = shift(held, "core", 1)
    return interleave(held, other, core).reshape(ys * cores * rows, n)


def activate(gate, upper):
    sig = jax.nn.sigmoid(gate)
    return (gate * sig * upper).astype(BF16)


def backprop(back, gate, upper):
    sig = jax.nn.sigmoid(gate)
    d_gate = (back * upper * sig * (1.0 + gate * (1.0 - sig))).astype(BF16)
    d_up = (back * gate * sig).astype(BF16)
    return d_gate, d_up


def body(tokens, cotangent, route, score, clusters, w_gate, w_up, w_down):
    experts = lax.axis_size(EXPERT)
    pair_cap = SLOTS // experts
    tok_count, width = tokens.shape
    tok_cap = 4 * tok_count // experts
    route, score, ids = route.T, score.T, clusters.T
    over_rows = (((0,), (0,)), ((), ()))

    sent = load(route, ids, tokens, w_gate, w_up, experts, tok_cap, pair_cap)
    raw = lax.all_to_all(sent, EXPERT, split_axis=0, concat_axis=0, tiled=True)
    packed_down = pack(ids, w_down, w_down, experts, pair_cap, width // 2, (0, 1))
    sent_grads = dispatch(route, score, cotangent, experts, tok_cap, True)
    raw_down = exchange(after(packed_down, (raw, sent_grads)), experts)
    rows_x, gate_up_rows = unload(raw, tok_cap, pair_cap)
    steps = scatter_start(product(rows_x, gate_up_rows, True))
    rows_dy = exchange(after(sent_grads, (raw_down, steps)), experts)
    terms = scatter_end(*steps)
    hidden, sums = hidden_of(terms)
    hidden = gather_blocks(hidden)
    down_rows = unpack_one(raw_down, pair_cap)
    out_part = product(hidden, down_rows, False)
    picks = token_pairs(route, experts, tok_cap)
    out_part, rows_dy, picks = lax.optimization_barrier((out_part, rows_dy, picks))
    back_out = exchange(out_part, experts)

    back = scatter_end(*scatter_start(product(rows_dy, down_rows, True)))
    d_both = gather_blocks(backprop_of(back, sums))
    input_part = product(d_both, gate_up_rows, False)
    back_in = exchange(after(input_part, back_out), experts)

    d_both, hidden, rows_dy = after((d_both, hidden, rows_dy), input_part)
    grad_down = lax.dot_general(hidden, rows_dy, over_rows, preferred_element_type=F32)
    grad_gate = lax.dot_general(
        d_both[:, :SLOTS], rows_x, over_rows, preferred_element_type=F32
    )
    grad_up = lax.dot_general(d_both[:, SLOTS:], rows_x, over_rows, preferred_element_type=F32)
    mixed = combine(route, score, back_out, experts, tok_cap)
    input_grad = pair_rows(picks, back_in)
    return (
        mixed,
        input_grad,
        grad_gate.astype(BF16)[None],
        grad_up.astype(BF16)[None],
        grad_down.astype(BF16)[None],
    )


def solution(mesh):
    fine = Mesh(mesh.devices.reshape(4, 2, 8, 4), DP + EXPERT)
    full, rows_only = P(EXPERT, DP), P(EXPERT, None)
    grads = P(EXPERT, None, DP)
    return jax.shard_map(
        body,
        mesh=fine,
        in_specs=(full, full, rows_only, rows_only, rows_only, full, full, full),
        out_specs=(full, full, grads, grads, grads),
        check_vma=False,
    )
```

```python
import functools

import jax
import jax.numpy as jnp
from jax import lax
from jax.experimental import pallas as pl
from jax.experimental.pallas import tpu as pltpu
from jax.sharding import Mesh
from jax.sharding import PartitionSpec as P

SLOTS = 640
EXPERT = ("z", "x")
DP = ("y", "core")
BF16 = jnp.bfloat16
F32 = jnp.float32
LIMIT = 48 * 1024 * 1024
MOST = 63 * 1024 * 1024
FREE = pl.CostEstimate(flops=0, bytes_accessed=0, transcendentals=0)


def iota(shape, axis):
    return lax.broadcasted_iota(jnp.int32, shape, axis)


def kernel_call(body, name, limit=LIMIT, **kwargs):
    return pl.pallas_call(
        body,
        name=name,
        compiler_params=pltpu.CompilerParams(vmem_limit_bytes=limit),
        **kwargs,
    )


def ranks(rows, count):
    n = rows[0].shape[1]
    hits = [iota((count, n), 0) == ids for ids in rows]
    seen = sum(hit.astype(F32) for hit in hits).astype(BF16)
    earlier = (iota((n, n), 0) < iota((n, n), 1)).astype(F32).astype(BF16)
    before = jnp.dot(seen, earlier, preferred_element_type=F32)
    return [
        jnp.sum(jnp.where(hit, before, 0.0), axis=0, keepdims=True).astype(jnp.int32)
        for hit in hits
    ]


def token_places(route_ref, experts, cap):
    rows = [route_ref[0:1, :], route_ref[1:2, :]]
    return [ids * cap + rank for ids, rank in zip(rows, ranks(rows, experts))]


def token_shares(score_ref):
    score = score_ref[...].astype(F32)
    first, second = score[0:1, :], score[1:2, :]
    total = first + second
    return first / total, second / total


def dispatch_body(scaled, experts, cap, *refs):
    route_ref, x_ref, out_ref = refs[0], refs[-2], refs[-1]
    block, count = out_ref.shape[0], x_ref.shape[0]
    places = token_places(route_ref, experts, cap)
    slot = iota((block, count), 0) + pl.program_id(0) * block
    hits = [slot == place for place in places]
    pick = jnp.where(hits[0] | hits[1], 1.0, 0.0).astype(BF16)
    rows = jnp.dot(pick, x_ref[...], preferred_element_type=F32)
    if scaled:
        shares = token_shares(refs[1])
        weight = jnp.where(hits[0], shares[0], 0.0) + jnp.where(hits[1], shares[1], 0.0)
        rows = rows * jnp.sum(weight, axis=1, keepdims=True)
    out_ref[...] = rows.astype(BF16)


def dispatch(route, score, x, experts, cap, scaled):
    count, width = x.shape
    block = 256
    total = experts * cap
    whole = lambda i: (0, 0)
    return kernel_call(
        functools.partial(dispatch_body, scaled, experts, cap),
        "dispatch",
        grid=(total // block,),
        in_specs=[pl.BlockSpec((2, count), whole)] * (2 if scaled else 1)
        + [pl.BlockSpec((count, width), whole)],
        out_specs=pl.BlockSpec((block, width), lambda i: (i, 0)),
        out_shape=jax.ShapeDtypeStruct((total, width), BF16),
    )(*((route, score) if scaled else (route,)), x)


def pack_body(experts, cap, ids_ref, a_ref, b_ref, out_ref):
    block, count = out_ref.shape[0], a_ref.shape[0]
    ids = ids_ref[...]
    place = ids * (2 * cap) + ranks([ids], experts)[0]
    slot = iota((block, count), 0) + pl.program_id(0) * block
    pick_a = jnp.where(slot == place, 1.0, 0.0).astype(BF16)
    pick_b = jnp.where(slot == place + cap, 1.0, 0.0).astype(BF16)
    out_ref[...] = (
        jnp.dot(pick_a, a_ref[...], preferred_element_type=F32)
        + jnp.dot(pick_b, b_ref[...], preferred_element_type=F32)
    ).astype(BF16)


def pack(ids, a, b, experts, cap, width, columns):
    count = a.shape[0]
    block = 256
    total = 2 * experts * cap
    whole = lambda i: (0, 0)
    return kernel_call(
        functools.partial(pack_body, experts, cap),
        "pack",
        grid=(total // block,),
        in_specs=[
            pl.BlockSpec((1, count), whole),
            pl.BlockSpec((count, width), lambda i: (0, columns[0])),
            pl.BlockSpec((count, width), lambda i: (0, columns[1])),
        ],
        out_specs=pl.BlockSpec((block, width), lambda i: (i, 0)),
        out_shape=jax.ShapeDtypeStruct((total, width), BF16),
    )(ids, a, b)


def load_body(experts, cap, pair_cap, route_ref, ids_ref, *refs):
    held_in, out_ref, token_at, row_at = refs[:3], refs[3], refs[4], refs[5]
    held, sems = refs[6:9], refs[9]
    per = out_ref.shape[0]
    first = pl.program_id(0) * per
    pairs = 2 * pair_cap

    @pl.when(pl.program_id(0) == 0)
    def _():
        copies = [
            pltpu.make_async_copy(source, target, sems.at[k])
            for k, (source, target) in enumerate(zip(held_in, held))
        ]
        for copy in copies:
            copy.start()
        for k, place in enumerate(token_places(route_ref, experts, cap)):
            token_at[k : k + 1, :] = place
        ids = ids_ref[...]
        row_at[0:1, :] = ids * pairs + ranks([ids], experts)[0]
        for copy in copies:
            copy.wait()

    x_ref, a_ref, b_ref = held
    places = [token_at[k : k + 1, :] for k in (0, 1)]
    slot = iota((per * cap, x_ref.shape[0]), 0) + first * cap
    pick = jnp.where((slot == places[0]) | (slot == places[1]), 1.0, 0.0).astype(BF16)
    tokens = jnp.dot(pick, x_ref[...], preferred_element_type=F32)
    place = row_at[0:1, :]
    slot = iota((per * pairs, a_ref.shape[0]), 0) + first * pairs
    pick_a = jnp.where(slot == place, 1.0, 0.0).astype(BF16)
    pick_b = jnp.where(slot == place + pair_cap, 1.0, 0.0).astype(BF16)
    weights = jnp.dot(pick_a, a_ref[...], preferred_element_type=F32) + jnp.dot(
        pick_b, b_ref[...], preferred_element_type=F32
    )
    for k in range(per):
        out_ref[k, :cap, :] = tokens[k * cap : (k + 1) * cap, :].astype(BF16)
        out_ref[k, cap:, :] = weights[k * pairs : (k + 1) * pairs, :].astype(BF16)


def load(route, ids, x, a, b, experts, cap, pair_cap):
    width = x.shape[1]
    per = 8
    whole = lambda i: (0, 0)
    return kernel_call(
        functools.partial(load_body, experts, cap, pair_cap),
        "load",
        MOST,
        grid=(experts // per,),
        in_specs=[pl.BlockSpec(v.shape, whole) for v in (route, ids)]
        + [pl.BlockSpec(memory_space=pltpu.HBM)] * 3,
        out_specs=pl.BlockSpec((per, cap + 2 * pair_cap, width), lambda i: (i, 0, 0)),
        out_shape=jax.ShapeDtypeStruct((experts, cap + 2 * pair_cap, width), BF16),
        scratch_shapes=[
            pltpu.VMEM((8, x.shape[0]), jnp.int32),
            pltpu.VMEM((8, a.shape[0]), jnp.int32),
        ]
        + [pltpu.VMEM(v.shape, v.dtype) for v in (x, a, b)]
        + [pltpu.SemaphoreType.DMA((3,))],
    )(route, ids, x, a, b)


def unload_body(cap, pair_cap, raw_ref, rows_ref, weights_ref):
    per = raw_ref.shape[0]
    for k in range(per):
        rows_ref[k * cap : (k + 1) * cap, :] = raw_ref[k, :cap, :]
    raw = jnp.concatenate(
        [raw_ref[k, cap:, :].astype(F32) for k in range(per)], axis=0
    ).astype(BF16)
    picks = unpack_picks(weights_ref.shape[1], pair_cap)
    for k in (0, 1):
        weights_ref[k] = jnp.dot(picks[k], raw, preferred_element_type=F32).astype(BF16)


def unload(raw, cap, pair_cap):
    experts, width = raw.shape[0], raw.shape[2]
    per = 8
    rows, weights = kernel_call(
        functools.partial(unload_body, cap, pair_cap),
        "unload",
        grid=(experts // per,),
        in_specs=[pl.BlockSpec((per,) + raw.shape[1:], lambda i: (i, 0, 0))],
        out_specs=[
            pl.BlockSpec((per * cap, width), lambda i: (i, 0)),
            pl.BlockSpec((2, per * pair_cap, width), lambda i: (0, i, 0)),
        ],
        out_shape=[
            jax.ShapeDtypeStruct((experts * cap, width), BF16),
            jax.ShapeDtypeStruct((2, experts * pair_cap, width), BF16),
        ],
    )(raw)
    return rows, weights.reshape(2 * experts * pair_cap, width)


def unpack_picks(block, cap):
    row, column = iota((block, 2 * block), 0), iota((block, 2 * block), 1)
    group = sum((row >= g * cap).astype(jnp.int32) for g in range(1, block // cap))
    first = row + cap * group
    return [jnp.where(column == first + k * cap, 1.0, 0.0).astype(BF16) for k in (0, 1)]


def unpack_one_body(cap, raw_ref, out_ref):
    width = raw_ref.shape[1]
    picks = unpack_picks(out_ref.shape[0], cap)
    raw = raw_ref[...]
    for k in (0, 1):
        out_ref[:, k * width : (k + 1) * width] = jnp.dot(
            picks[k], raw, preferred_element_type=F32
        ).astype(BF16)


def unpack_one(raw, cap):
    rows, width = raw.shape[0] // 2, raw.shape[1]
    block = 160
    return kernel_call(
        functools.partial(unpack_one_body, cap),
        "unpack_one",
        grid=(rows // block,),
        in_specs=[pl.BlockSpec((2 * block, width), lambda i: (i, 0))],
        out_specs=pl.BlockSpec((block, 2 * width), lambda i: (i, 0)),
        out_shape=jax.ShapeDtypeStruct((rows, 2 * width), BF16),
    )(raw)


def add_half_body(start, rows_ref, half_ref, out_ref):
    width = half_ref.shape[1]
    out_ref[...] = rows_ref[...]
    side = (slice(None), slice(start, start + width))
    out_ref[side] = (rows_ref[side].astype(F32) + half_ref[...].astype(F32)).astype(BF16)


def add_half(rows, half, start):
    return kernel_call(
        functools.partial(add_half_body, start),
        "add_half",
        out_shape=jax.ShapeDtypeStruct(rows.shape, BF16),
        cost_estimate=FREE,
    )(rows, half)


def sum_three(refs):
    return sum(ref[...].astype(F32) for ref in refs)


def hidden_body(own_ref, below_ref, above_ref, hidden_ref, sums_ref):
    sums = sum_three((own_ref, below_ref, above_ref))
    sums_ref[...] = sums
    hidden_ref[...] = activate(sums[:, :SLOTS], sums[:, SLOTS:])


def hidden_of(parts):
    rows, n = parts[0].shape
    return kernel_call(
        hidden_body,
        "hidden",
        out_shape=[
            jax.ShapeDtypeStruct((rows, n // 2), BF16),
            jax.ShapeDtypeStruct((rows, n), F32),
        ],
        cost_estimate=FREE,
    )(*parts)


def backprop_body(own_ref, below_ref, above_ref, sums_ref, out_ref):
    back = sum_three((own_ref, below_ref, above_ref))
    d_gate, d_up = backprop(back, sums_ref[:, :SLOTS], sums_ref[:, SLOTS:])
    out_ref[:, :SLOTS] = d_gate
    out_ref[:, SLOTS:] = d_up


def backprop_of(parts, sums):
    return kernel_call(
        backprop_body,
        "backprop",
        out_shape=jax.ShapeDtypeStruct(sums.shape, BF16),
        cost_estimate=FREE,
    )(*parts, sums)


def interleave_body(core_ref, own_ref, other_ref, out_ref):
    core = core_ref[0]
    out_ref[:, core] = own_ref[...]
    out_ref[:, 1 - core] = other_ref[...]


def interleave(own, other, core):
    ys, rows, n = own.shape
    return kernel_call(
        interleave_body,
        "interleave",
        in_specs=[
            pl.BlockSpec(memory_space=pltpu.SMEM),
            pl.BlockSpec(memory_space=pltpu.VMEM),
            pl.BlockSpec(memory_space=pltpu.VMEM),
        ],
        out_shape=jax.ShapeDtypeStruct((ys, 2, rows, n), own.dtype),
        cost_estimate=FREE,
    )(core[None], own, other)


def pair_body(core_ref, value_ref, other_ref, out_ref):
    own = value_ref[:, core_ref[0]]
    out_ref[...] = (own.astype(F32) + other_ref[...].astype(F32)).astype(BF16)


def pair_sum(core, value, other):
    vmem = pl.BlockSpec(memory_space=pltpu.VMEM)
    return kernel_call(
        pair_body,
        "pair_sum",
        in_specs=[pl.BlockSpec(memory_space=pltpu.SMEM), vmem, vmem],
        out_shape=jax.ShapeDtypeStruct(other.shape, BF16),
        cost_estimate=FREE,
    )(core[None], value, other)


def column_body(y_ref, own_ref, below_ref, above_ref, low_ref, high_ref, out_ref):
    ys, half = out_ref.shape[0], low_ref.shape[1]
    y = y_ref[0]
    out_ref[y] = own_ref[...]
    out_ref[lax.rem(y + ys - 1, ys)] = below_ref[...]
    out_ref[lax.rem(y + 1, ys)] = above_ref[...]
    far = lax.rem(y + 2, ys)
    out_ref[far, :, :half] = low_ref[...]
    out_ref[far, :, half:] = high_ref[...]


def column(y, own, below, above, low, high):
    ys = lax.axis_size("y")
    vmem = pl.BlockSpec(memory_space=pltpu.VMEM)
    return kernel_call(
        column_body,
        "column",
        in_specs=[pl.BlockSpec(memory_space=pltpu.SMEM)] + [vmem] * 5,
        out_shape=jax.ShapeDtypeStruct((ys,) + own.shape, own.dtype),
        cost_estimate=FREE,
    )(y[None], own, below, above, low, high)


def product_body(dims, a_ref, b_ref, out_ref):
    out_ref[...] = lax.dot_general(
        a_ref[...], b_ref[...], dims, preferred_element_type=F32
    ).astype(BF16)


def product(a, b, transposed):
    rows, depth = a.shape
    n = b.shape[0 if transposed else 1]
    block = 512
    dims = (((1,), (1 if transposed else 0,)), ((), ()))
    return kernel_call(
        functools.partial(product_body, dims),
        "product",
        grid=(rows // block,),
        in_specs=[
            pl.BlockSpec((block, depth), lambda i: (i, 0)),
            pl.BlockSpec(b.shape, lambda i: (0, 0)),
        ],
        out_specs=pl.BlockSpec((block, n), lambda i: (i, 0)),
        out_shape=jax.ShapeDtypeStruct((rows, n), BF16),
        cost_estimate=FREE,
    )(a, b)


def column_of(row):
    n = row.shape[1]
    same = iota((n, n), 0) == iota((n, n), 1)
    return jnp.sum(jnp.where(same, row, jnp.zeros_like(row)), axis=1, keepdims=True)


def combine_body(experts, cap, route_ref, score_ref, rows_ref, out_ref):
    count, total = out_ref.shape[0], rows_ref.shape[0]
    places = [column_of(place) for place in token_places(route_ref, experts, cap)]
    slot = iota((count, total), 1)
    hits = [slot == place for place in places]
    rows = rows_ref[...]
    shares = [column_of(share) for share in token_shares(score_ref)]
    weight = jnp.where(hits[0], shares[0], 0.0) + jnp.where(hits[1], shares[1], 0.0)
    high = weight.astype(BF16)
    low = (weight - high.astype(F32)).astype(BF16)
    out_ref[...] = (
        jnp.dot(high, rows, preferred_element_type=F32)
        + jnp.dot(low, rows, preferred_element_type=F32)
    ).astype(BF16)


def combine(route, score, rows, experts, cap):
    count = route.shape[1]
    total, width = rows.shape
    block = 512
    whole = lambda i: (0, 0)
    return kernel_call(
        functools.partial(combine_body, experts, cap),
        "combine",
        grid=(width // block,),
        in_specs=[pl.BlockSpec((2, count), whole)] * 2
        + [pl.BlockSpec((total, block), lambda i: (0, i))],
        out_specs=pl.BlockSpec((count, block), lambda i: (0, i)),
        out_shape=jax.ShapeDtypeStruct((count, width), BF16),
    )(route, score, rows)


def pairs_body(experts, cap, route_ref, out_ref):
    places = [column_of(place) for place in token_places(route_ref, experts, cap)]
    slot = iota(out_ref.shape, 1)
    out_ref[...] = jnp.where((slot == places[0]) | (slot == places[1]), 1.0, 0.0).astype(BF16)


def token_pairs(route, experts, cap):
    return kernel_call(
        functools.partial(pairs_body, experts, cap),
        "token_pairs",
        out_shape=jax.ShapeDtypeStruct((route.shape[1], experts * cap), BF16),
    )(route)


def pair_rows_body(parts, picks_in, rows_in, out_ref, picks, rows, sems):
    block = rows.shape[0] // parts
    copies = [pltpu.make_async_copy(picks_in, picks, sems.at[parts])]
    for k in range(parts):
        some = pl.ds(k * block, block)
        copies.append(pltpu.make_async_copy(rows_in.at[some], rows.at[some], sems.at[k]))
    for copy in copies:
        copy.start()
    copies[0].wait()
    total = None
    for k in range(parts):
        copies[k + 1].wait()
        some = slice(k * block, (k + 1) * block)
        term = jnp.dot(picks[:, some], rows[some, :], preferred_element_type=F32)
        total = term if total is None else total + term
    out_ref[...] = total.astype(BF16)


def pair_rows(picks, rows):
    parts = 4
    held = pl.BlockSpec(memory_space=pltpu.HBM)
    return kernel_call(
        functools.partial(pair_rows_body, parts),
        "pair_rows",
        MOST,
        in_specs=[held, held],
        out_specs=pl.BlockSpec(memory_space=pltpu.VMEM),
        out_shape=jax.ShapeDtypeStruct((picks.shape[0], rows.shape[1]), BF16),
        scratch_shapes=[
            pltpu.VMEM(picks.shape, BF16),
            pltpu.VMEM(rows.shape, BF16),
            pltpu.SemaphoreType.DMA((parts + 1,)),
        ],
    )(picks, rows)


def exchange(rows, parts):
    total, width = rows.shape
    return lax.all_to_all(
        rows.reshape(parts, total // parts, width),
        EXPERT,
        split_axis=0,
        concat_axis=0,
        tiled=True,
    ).reshape(total, width)


def after(value, other):
    return lax.optimization_barrier((value, other))[0]


def shift(value, axis, step):
    size = lax.axis_size(axis)
    return lax.ppermute(value, axis, [(i, (i + step) % size) for i in range(size)])


def pick(value, index, axis):
    return lax.dynamic_index_in_dim(value, index, axis, keepdims=False)


def put(value, part, y, core):
    return lax.dynamic_update_slice(value, part[None, None], (y, core, 0, 0))


def scatter_start(value):
    rows, n = value.shape
    ys, cores = lax.axis_size("y"), lax.axis_size("core")
    y, core = lax.axis_index("y"), lax.axis_index("core")
    value = value.reshape(ys, cores, rows // (ys * cores), n)
    other = shift(pick(value, 1 - core, 1), "core", 1)
    pair = pair_sum(core, value, other)
    half = n // 256 * 128
    far = pick(pair, (y + 2) % ys, 0)
    low = shift(far[:, :half], "y", 1)
    high = shift(far[:, half:], "y", -1)
    to_above = add_half(pick(pair, (y + 1) % ys, 0), low, 0)
    to_below = add_half(pick(pair, (y + ys - 1) % ys, 0), high, half)
    return pick(pair, y, 0), to_above, to_below


def scatter_end(own, to_above, to_below):
    return own, shift(to_above, "y", 1), shift(to_below, "y", -1)


def gather_blocks(part):
    rows, n = part.shape
    ys, cores = lax.axis_size("y"), lax.axis_size("core")
    y, core = lax.axis_index("y"), lax.axis_index("core")
    half = n // 256 * 128
    from_below = shift(part, "y", 1)
    from_above = shift(part, "y", -1)
    low = shift(from_below[:, :half], "y", 1)
    high = shift(from_above[:, half:], "y", -1)
    held = column(y, part, from_below, from_above, low, high)
    other = shift(held, "core", 1)
    return interleave(held, other, core).reshape(ys * cores * rows, n)


def activate(gate, upper):
    sig = jax.nn.sigmoid(gate)
    return (gate * sig * upper).astype(BF16)


def backprop(back, gate, upper):
    sig = jax.nn.sigmoid(gate)
    d_gate = (back * upper * sig * (1.0 + gate * (1.0 - sig))).astype(BF16)
    d_up = (back * gate * sig).astype(BF16)
    return d_gate, d_up


def body(tokens, cotangent, route, score, clusters, w_gate, w_up, w_down):
    experts = lax.axis_size(EXPERT)
    pair_cap = SLOTS // experts
    tok_count, width = tokens.shape
    tok_cap = 4 * tok_count // experts
    route, score, ids = route.T, score.T, clusters.T
    over_rows = (((0,), (0,)), ((), ()))

    sent = load(route, ids, tokens, w_gate, w_up, experts, tok_cap, pair_cap)
    raw = lax.all_to_all(sent, EXPERT, split_axis=0, concat_axis=0, tiled=True)
    packed_down = pack(ids, w_down, w_down, experts, pair_cap, width // 2, (0, 1))
    sent_grads = dispatch(route, score, cotangent, experts, tok_cap, True)
    raw_down = exchange(after(packed_down, (raw, sent_grads)), experts)
    rows_x, gate_up_rows = unload(raw, tok_cap, pair_cap)
    steps = scatter_start(product(rows_x, gate_up_rows, True))
    rows_dy = exchange(after(sent_grads, (raw_down, steps)), experts)
    terms = scatter_end(*steps)
    hidden, sums = hidden_of(terms)
    hidden = gather_blocks(hidden)
    down_rows = unpack_one(raw_down, pair_cap)
    out_part = product(hidden, down_rows, False)
    picks = token_pairs(route, experts, tok_cap)
    out_part, rows_dy, picks = lax.optimization_barrier((out_part, rows_dy, picks))
    back_out = exchange(out_part, experts)

    back = scatter_end(*scatter_start(product(rows_dy, down_rows, True)))
    d_both = gather_blocks(backprop_of(back, sums))
    input_part = product(d_both, gate_up_rows, False)
    back_in = exchange(after(input_part, back_out), experts)

    d_both, hidden, rows_dy = after((d_both, hidden, rows_dy), input_part)
    grad_down = lax.dot_general(hidden, rows_dy, over_rows, preferred_element_type=F32)
    grad_gate = lax.dot_general(
        d_both[:, :SLOTS], rows_x, over_rows, preferred_element_type=F32
    )
    grad_up = lax.dot_general(d_both[:, SLOTS:], rows_x, over_rows, preferred_element_type=F32)
    mixed = combine(route, score, back_out, experts, tok_cap)
    input_grad = pair_rows(picks, back_in)
    return (
        mixed,
        input_grad,
        grad_gate.astype(BF16)[None],
        grad_up.astype(BF16)[None],
        grad_down.astype(BF16)[None],
    )


def solution(mesh):
    fine = Mesh(mesh.devices.reshape(4, 2, 8, 4), DP + EXPERT)
    full, rows_only = P(EXPERT, DP), P(EXPERT, None)
    grads = P(EXPERT, None, DP)
    return jax.shard_map(
        body,
        mesh=fine,
        in_specs=(full, full, rows_only, rows_only, rows_only, full, full, full),
        out_specs=(full, full, grads, grads, grads),
        check_vma=False,
    )
```

```python
import functools

import jax
import jax.numpy as jnp
from jax import lax
from jax.experimental import pallas as pl
from jax.experimental.pallas import tpu as pltpu
from jax.sharding import Mesh
from jax.sharding import PartitionSpec as P

SLOTS = 640
EXPERT = ("z", "x")
DP = ("y", "core")
BF16 = jnp.bfloat16
F32 = jnp.float32
LIMIT = 48 * 1024 * 1024
MOST = 63 * 1024 * 1024
FREE = pl.CostEstimate(flops=0, bytes_accessed=0, transcendentals=0)


def iota(shape, axis):
    return lax.broadcasted_iota(jnp.int32, shape, axis)


def kernel_call(body, name, limit=LIMIT, **kwargs):
    return pl.pallas_call(
        body,
        name=name,
        compiler_params=pltpu.CompilerParams(vmem_limit_bytes=limit),
        **kwargs,
    )


def ranks(rows, count):
    n = rows[0].shape[1]
    hits = [iota((count, n), 0) == ids for ids in rows]
    seen = sum(hit.astype(F32) for hit in hits).astype(BF16)
    earlier = (iota((n, n), 0) < iota((n, n), 1)).astype(F32).astype(BF16)
    before = jnp.dot(seen, earlier, preferred_element_type=F32)
    return [
        jnp.sum(jnp.where(hit, before, 0.0), axis=0, keepdims=True).astype(jnp.int32)
        for hit in hits
    ]


def token_places(route_ref, experts, cap):
    rows = [route_ref[0:1, :], route_ref[1:2, :]]
    return [ids * cap + rank for ids, rank in zip(rows, ranks(rows, experts))]


def token_shares(score_ref):
    score = score_ref[...].astype(F32)
    first, second = score[0:1, :], score[1:2, :]
    total = first + second
    return first / total, second / total


def dispatch_body(scaled, experts, cap, *refs):
    route_ref, x_ref, out_ref = refs[0], refs[-2], refs[-1]
    block, count = out_ref.shape[0], x_ref.shape[0]
    places = token_places(route_ref, experts, cap)
    slot = iota((block, count), 0) + pl.program_id(0) * block
    hits = [slot == place for place in places]
    pick = jnp.where(hits[0] | hits[1], 1.0, 0.0).astype(BF16)
    rows = jnp.dot(pick, x_ref[...], preferred_element_type=F32)
    if scaled:
        shares = token_shares(refs[1])
        weight = jnp.where(hits[0], shares[0], 0.0) + jnp.where(hits[1], shares[1], 0.0)
        rows = rows * jnp.sum(weight, axis=1, keepdims=True)
    out_ref[...] = rows.astype(BF16)


def dispatch(route, score, x, experts, cap, scaled):
    count, width = x.shape
    block = 256
    total = experts * cap
    whole = lambda i: (0, 0)
    return kernel_call(
        functools.partial(dispatch_body, scaled, experts, cap),
        "dispatch",
        grid=(total // block,),
        in_specs=[pl.BlockSpec((2, count), whole)] * (2 if scaled else 1)
        + [pl.BlockSpec((count, width), whole)],
        out_specs=pl.BlockSpec((block, width), lambda i: (i, 0)),
        out_shape=jax.ShapeDtypeStruct((total, width), BF16),
    )(*((route, score) if scaled else (route,)), x)


def pack_body(experts, cap, ids_ref, a_ref, b_ref, out_ref):
    block, count = out_ref.shape[0], a_ref.shape[0]
    ids = ids_ref[...]
    place = ids * (2 * cap) + ranks([ids], experts)[0]
    slot = iota((block, count), 0) + pl.program_id(0) * block
    pick_a = jnp.where(slot == place, 1.0, 0.0).astype(BF16)
    pick_b = jnp.where(slot == place + cap, 1.0, 0.0).astype(BF16)
    out_ref[...] = (
        jnp.dot(pick_a, a_ref[...], preferred_element_type=F32)
        + jnp.dot(pick_b, b_ref[...], preferred_element_type=F32)
    ).astype(BF16)


def pack(ids, a, b, experts, cap, width, columns):
    count = a.shape[0]
    block = 256
    total = 2 * experts * cap
    whole = lambda i: (0, 0)
    return kernel_call(
        functools.partial(pack_body, experts, cap),
        "pack",
        grid=(total // block,),
        in_specs=[
            pl.BlockSpec((1, count), whole),
            pl.BlockSpec((count, width), lambda i: (0, columns[0])),
            pl.BlockSpec((count, width), lambda i: (0, columns[1])),
        ],
        out_specs=pl.BlockSpec((block, width), lambda i: (i, 0)),
        out_shape=jax.ShapeDtypeStruct((total, width), BF16),
    )(ids, a, b)


def load_body(experts, cap, pair_cap, route_ref, ids_ref, *refs):
    held_in, out_ref, token_at, row_at = refs[:3], refs[3], refs[4], refs[5]
    held, sems = refs[6:9], refs[9]
    per = out_ref.shape[0]
    first = pl.program_id(0) * per
    pairs = 2 * pair_cap

    @pl.when(pl.program_id(0) == 0)
    def _():
        copies = [
            pltpu.make_async_copy(source, target, sems.at[k])
            for k, (source, target) in enumerate(zip(held_in, held))
        ]
        for copy in copies:
            copy.start()
        for k, place in enumerate(token_places(route_ref, experts, cap)):
            token_at[k : k + 1, :] = place
        ids = ids_ref[...]
        row_at[0:1, :] = ids * pairs + ranks([ids], experts)[0]
        for copy in copies:
            copy.wait()

    x_ref, a_ref, b_ref = held
    places = [token_at[k : k + 1, :] for k in (0, 1)]
    slot = iota((per * cap, x_ref.shape[0]), 0) + first * cap
    pick = jnp.where((slot == places[0]) | (slot == places[1]), 1.0, 0.0).astype(BF16)
    tokens = jnp.dot(pick, x_ref[...], preferred_element_type=F32)
    place = row_at[0:1, :]
    slot = iota((per * pairs, a_ref.shape[0]), 0) + first * pairs
    pick_a = jnp.where(slot == place, 1.0, 0.0).astype(BF16)
    pick_b = jnp.where(slot == place + pair_cap, 1.0, 0.0).astype(BF16)
    weights = jnp.dot(pick_a, a_ref[...], preferred_element_type=F32) + jnp.dot(
        pick_b, b_ref[...], preferred_element_type=F32
    )
    for k in range(per):
        out_ref[k, :cap, :] = tokens[k * cap : (k + 1) * cap, :].astype(BF16)
        out_ref[k, cap:, :] = weights[k * pairs : (k + 1) * pairs, :].astype(BF16)


def load(route, ids, x, a, b, experts, cap, pair_cap):
    width = x.shape[1]
    per = 8
    whole = lambda i: (0, 0)
    return kernel_call(
        functools.partial(load_body, experts, cap, pair_cap),
        "load",
        MOST,
        grid=(experts // per,),
        in_specs=[pl.BlockSpec(v.shape, whole) for v in (route, ids)]
        + [pl.BlockSpec(memory_space=pltpu.HBM)] * 3,
        out_specs=pl.BlockSpec((per, cap + 2 * pair_cap, width), lambda i: (i, 0, 0)),
        out_shape=jax.ShapeDtypeStruct((experts, cap + 2 * pair_cap, width), BF16),
        scratch_shapes=[
            pltpu.VMEM((8, x.shape[0]), jnp.int32),
            pltpu.VMEM((8, a.shape[0]), jnp.int32),
        ]
        + [pltpu.VMEM(v.shape, v.dtype) for v in (x, a, b)]
        + [pltpu.SemaphoreType.DMA((3,))],
    )(route, ids, x, a, b)


def unload_body(cap, pair_cap, raw_ref, rows_ref, weights_ref):
    per = raw_ref.shape[0]
    for k in range(per):
        rows_ref[k * cap : (k + 1) * cap, :] = raw_ref[k, :cap, :]
    raw = jnp.concatenate(
        [raw_ref[k, cap:, :].astype(F32) for k in range(per)], axis=0
    ).astype(BF16)
    picks = unpack_picks(weights_ref.shape[1], pair_cap)
    for k in (0, 1):
        weights_ref[k] = jnp.dot(picks[k], raw, preferred_element_type=F32).astype(BF16)


def unload(raw, cap, pair_cap):
    experts, width = raw.shape[0], raw.shape[2]
    per = 8
    rows, weights = kernel_call(
        functools.partial(unload_body, cap, pair_cap),
        "unload",
        grid=(experts // per,),
        in_specs=[pl.BlockSpec((per,) + raw.shape[1:], lambda i: (i, 0, 0))],
        out_specs=[
            pl.BlockSpec((per * cap, width), lambda i: (i, 0)),
            pl.BlockSpec((2, per * pair_cap, width), lambda i: (0, i, 0)),
        ],
        out_shape=[
            jax.ShapeDtypeStruct((experts * cap, width), BF16),
            jax.ShapeDtypeStruct((2, experts * pair_cap, width), BF16),
        ],
    )(raw)
    return rows, weights.reshape(2 * experts * pair_cap, width)


def unpack_picks(block, cap):
    row, column = iota((block, 2 * block), 0), iota((block, 2 * block), 1)
    group = sum((row >= g * cap).astype(jnp.int32) for g in range(1, block // cap))
    first = row + cap * group
    return [jnp.where(column == first + k * cap, 1.0, 0.0).astype(BF16) for k in (0, 1)]


def unpack_one_body(cap, raw_ref, out_ref):
    width = raw_ref.shape[1]
    picks = unpack_picks(out_ref.shape[0], cap)
    raw = raw_ref[...]
    for k in (0, 1):
        out_ref[:, k * width : (k + 1) * width] = jnp.dot(
            picks[k], raw, preferred_element_type=F32
        ).astype(BF16)


def unpack_one(raw, cap):
    rows, width = raw.shape[0] // 2, raw.shape[1]
    block = 160
    return kernel_call(
        functools.partial(unpack_one_body, cap),
        "unpack_one",
        grid=(rows // block,),
        in_specs=[pl.BlockSpec((2 * block, width), lambda i: (i, 0))],
        out_specs=pl.BlockSpec((block, 2 * width), lambda i: (i, 0)),
        out_shape=jax.ShapeDtypeStruct((rows, 2 * width), BF16),
    )(raw)


def add_half_body(start, rows_ref, half_ref, out_ref):
    width = half_ref.shape[1]
    out_ref[...] = rows_ref[...]
    side = (slice(None), slice(start, start + width))
    out_ref[side] = (rows_ref[side].astype(F32) + half_ref[...].astype(F32)).astype(BF16)


def add_half(rows, half, start):
    return kernel_call(
        functools.partial(add_half_body, start),
        "add_half",
        out_shape=jax.ShapeDtypeStruct(rows.shape, BF16),
        cost_estimate=FREE,
    )(rows, half)


def sum_three(refs):
    return sum(ref[...].astype(F32) for ref in refs)


def hidden_body(own_ref, below_ref, above_ref, hidden_ref, sums_ref):
    sums = sum_three((own_ref, below_ref, above_ref))
    sums_ref[...] = sums
    hidden_ref[...] = activate(sums[:, :SLOTS], sums[:, SLOTS:])


def hidden_of(parts):
    rows, n = parts[0].shape
    return kernel_call(
        hidden_body,
        "hidden",
        out_shape=[
            jax.ShapeDtypeStruct((rows, n // 2), BF16),
            jax.ShapeDtypeStruct((rows, n), F32),
        ],
        cost_estimate=FREE,
    )(*parts)


def backprop_body(own_ref, below_ref, above_ref, sums_ref, out_ref):
    back = sum_three((own_ref, below_ref, above_ref))
    d_gate, d_up = backprop(back, sums_ref[:, :SLOTS], sums_ref[:, SLOTS:])
    out_ref[:, :SLOTS] = d_gate
    out_ref[:, SLOTS:] = d_up


def backprop_of(parts, sums):
    return kernel_call(
        backprop_body,
        "backprop",
        out_shape=jax.ShapeDtypeStruct(sums.shape, BF16),
        cost_estimate=FREE,
    )(*parts, sums)


def interleave_body(core_ref, own_ref, other_ref, out_ref):
    core = core_ref[0]
    out_ref[:, core] = own_ref[...]
    out_ref[:, 1 - core] = other_ref[...]


def interleave(own, other, core):
    ys, rows, n = own.shape
    return kernel_call(
        interleave_body,
        "interleave",
        in_specs=[
            pl.BlockSpec(memory_space=pltpu.SMEM),
            pl.BlockSpec(memory_space=pltpu.VMEM),
            pl.BlockSpec(memory_space=pltpu.VMEM),
        ],
        out_shape=jax.ShapeDtypeStruct((ys, 2, rows, n), own.dtype),
        cost_estimate=FREE,
    )(core[None], own, other)


def pair_body(core_ref, value_ref, other_ref, out_ref):
    own = value_ref[:, core_ref[0]]
    out_ref[...] = (own.astype(F32) + other_ref[...].astype(F32)).astype(BF16)


def pair_sum(core, value, other):
    vmem = pl.BlockSpec(memory_space=pltpu.VMEM)
    return kernel_call(
        pair_body,
        "pair_sum",
        in_specs=[pl.BlockSpec(memory_space=pltpu.SMEM), vmem, vmem],
        out_shape=jax.ShapeDtypeStruct(other.shape, BF16),
        cost_estimate=FREE,
    )(core[None], value, other)


def column_body(y_ref, own_ref, below_ref, above_ref, low_ref, high_ref, out_ref):
    ys, half = out_ref.shape[0], low_ref.shape[1]
    y = y_ref[0]
    out_ref[y] = own_ref[...]
    out_ref[lax.rem(y + ys - 1, ys)] = below_ref[...]
    out_ref[lax.rem(y + 1, ys)] = above_ref[...]
    far = lax.rem(y + 2, ys)
    out_ref[far, :, :half] = low_ref[...]
    out_ref[far, :, half:] = high_ref[...]


def column(y, own, below, above, low, high):
    ys = lax.axis_size("y")
    vmem = pl.BlockSpec(memory_space=pltpu.VMEM)
    return kernel_call(
        column_body,
        "column",
        in_specs=[pl.BlockSpec(memory_space=pltpu.SMEM)] + [vmem] * 5,
        out_shape=jax.ShapeDtypeStruct((ys,) + own.shape, own.dtype),
        cost_estimate=FREE,
    )(y[None], own, below, above, low, high)


def product_body(dims, a_ref, b_ref, out_ref):
    out_ref[...] = lax.dot_general(
        a_ref[...], b_ref[...], dims, preferred_element_type=F32
    ).astype(BF16)


def product(a, b, transposed):
    rows, depth = a.shape
    n = b.shape[0 if transposed else 1]
    block = 1024
    dims = (((1,), (1 if transposed else 0,)), ((), ()))
    return kernel_call(
        functools.partial(product_body, dims),
        "product",
        grid=(rows // block,),
        in_specs=[
            pl.BlockSpec((block, depth), lambda i: (i, 0)),
            pl.BlockSpec(b.shape, lambda i: (0, 0)),
        ],
        out_specs=pl.BlockSpec((block, n), lambda i: (i, 0)),
        out_shape=jax.ShapeDtypeStruct((rows, n), BF16),
        cost_estimate=FREE,
    )(a, b)


def column_of(row):
    n = row.shape[1]
    same = iota((n, n), 0) == iota((n, n), 1)
    return jnp.sum(jnp.where(same, row, jnp.zeros_like(row)), axis=1, keepdims=True)


def combine_body(experts, cap, route_ref, score_ref, rows_ref, out_ref):
    count, total = out_ref.shape[0], rows_ref.shape[0]
    places = [column_of(place) for place in token_places(route_ref, experts, cap)]
    slot = iota((count, total), 1)
    hits = [slot == place for place in places]
    rows = rows_ref[...]
    shares = [column_of(share) for share in token_shares(score_ref)]
    weight = jnp.where(hits[0], shares[0], 0.0) + jnp.where(hits[1], shares[1], 0.0)
    high = weight.astype(BF16)
    low = (weight - high.astype(F32)).astype(BF16)
    out_ref[...] = (
        jnp.dot(high, rows, preferred_element_type=F32)
        + jnp.dot(low, rows, preferred_element_type=F32)
    ).astype(BF16)


def combine(route, score, rows, experts, cap):
    count = route.shape[1]
    total, width = rows.shape
    block = 512
    whole = lambda i: (0, 0)
    return kernel_call(
        functools.partial(combine_body, experts, cap),
        "combine",
        grid=(width // block,),
        in_specs=[pl.BlockSpec((2, count), whole)] * 2
        + [pl.BlockSpec((total, block), lambda i: (0, i))],
        out_specs=pl.BlockSpec((count, block), lambda i: (0, i)),
        out_shape=jax.ShapeDtypeStruct((count, width), BF16),
    )(route, score, rows)


def pairs_body(experts, cap, route_ref, out_ref):
    places = [column_of(place) for place in token_places(route_ref, experts, cap)]
    slot = iota(out_ref.shape, 1)
    out_ref[...] = jnp.where((slot == places[0]) | (slot == places[1]), 1.0, 0.0).astype(BF16)


def token_pairs(route, experts, cap):
    return kernel_call(
        functools.partial(pairs_body, experts, cap),
        "token_pairs",
        out_shape=jax.ShapeDtypeStruct((route.shape[1], experts * cap), BF16),
    )(route)


def pair_rows_body(parts, picks_in, rows_in, out_ref, picks, rows, sems):
    block = rows.shape[0] // parts
    copies = [pltpu.make_async_copy(picks_in, picks, sems.at[parts])]
    for k in range(parts):
        some = pl.ds(k * block, block)
        copies.append(pltpu.make_async_copy(rows_in.at[some], rows.at[some], sems.at[k]))
    for copy in copies:
        copy.start()
    copies[0].wait()
    total = None
    for k in range(parts):
        copies[k + 1].wait()
        some = slice(k * block, (k + 1) * block)
        term = jnp.dot(picks[:, some], rows[some, :], preferred_element_type=F32)
        total = term if total is None else total + term
    out_ref[...] = total.astype(BF16)


def pair_rows(picks, rows):
    parts = 4
    held = pl.BlockSpec(memory_space=pltpu.HBM)
    return kernel_call(
        functools.partial(pair_rows_body, parts),
        "pair_rows",
        MOST,
        in_specs=[held, held],
        out_specs=pl.BlockSpec(memory_space=pltpu.VMEM),
        out_shape=jax.ShapeDtypeStruct((picks.shape[0], rows.shape[1]), BF16),
        scratch_shapes=[
            pltpu.VMEM(picks.shape, BF16),
            pltpu.VMEM(rows.shape, BF16),
            pltpu.SemaphoreType.DMA((parts + 1,)),
        ],
    )(picks, rows)


def exchange(rows, parts):
    total, width = rows.shape
    return lax.all_to_all(
        rows.reshape(parts, total // parts, width),
        EXPERT,
        split_axis=0,
        concat_axis=0,
        tiled=True,
    ).reshape(total, width)


def after(value, other):
    return lax.optimization_barrier((value, other))[0]


def shift(value, axis, step):
    size = lax.axis_size(axis)
    return lax.ppermute(value, axis, [(i, (i + step) % size) for i in range(size)])


def pick(value, index, axis):
    return lax.dynamic_index_in_dim(value, index, axis, keepdims=False)


def put(value, part, y, core):
    return lax.dynamic_update_slice(value, part[None, None], (y, core, 0, 0))


def scatter_start(value):
    rows, n = value.shape
    ys, cores = lax.axis_size("y"), lax.axis_size("core")
    y, core = lax.axis_index("y"), lax.axis_index("core")
    value = value.reshape(ys, cores, rows // (ys * cores), n)
    other = shift(pick(value, 1 - core, 1), "core", 1)
    pair = pair_sum(core, value, other)
    half = n // 256 * 128
    far = pick(pair, (y + 2) % ys, 0)
    low = shift(far[:, :half], "y", 1)
    high = shift(far[:, half:], "y", -1)
    to_above = add_half(pick(pair, (y + 1) % ys, 0), low, 0)
    to_below = add_half(pick(pair, (y + ys - 1) % ys, 0), high, half)
    return pick(pair, y, 0), to_above, to_below


def scatter_end(own, to_above, to_below):
    return own, shift(to_above, "y", 1), shift(to_below, "y", -1)


def gather_blocks(part):
    rows, n = part.shape
    ys, cores = lax.axis_size("y"), lax.axis_size("core")
    y, core = lax.axis_index("y"), lax.axis_index("core")
    half = n // 256 * 128
    from_below = shift(part, "y", 1)
    from_above = shift(part, "y", -1)
    low = shift(from_below[:, :half], "y", 1)
    high = shift(from_above[:, half:], "y", -1)
    held = column(y, part, from_below, from_above, low, high)
    other = shift(held, "core", 1)
    return interleave(held, other, core).reshape(ys * cores * rows, n)


def activate(gate, upper):
    sig = jax.nn.sigmoid(gate)
    return (gate * sig * upper).astype(BF16)


def backprop(back, gate, upper):
    sig = jax.nn.sigmoid(gate)
    d_gate = (back * upper * sig * (1.0 + gate * (1.0 - sig))).astype(BF16)
    d_up = (back * gate * sig).astype(BF16)
    return d_gate, d_up


def body(tokens, cotangent, route, score, clusters, w_gate, w_up, w_down):
    experts = lax.axis_size(EXPERT)
    pair_cap = SLOTS // experts
    tok_count, width = tokens.shape
    tok_cap = 4 * tok_count // experts
    route, score, ids = route.T, score.T, clusters.T
    over_rows = (((0,), (0,)), ((), ()))

    sent = load(route, ids, tokens, w_gate, w_up, experts, tok_cap, pair_cap)
    raw = lax.all_to_all(sent, EXPERT, split_axis=0, concat_axis=0, tiled=True)
    packed_down = pack(ids, w_down, w_down, experts, pair_cap, width // 2, (0, 1))
    sent_grads = dispatch(route, score, cotangent, experts, tok_cap, True)
    raw_down = exchange(after(packed_down, (raw, sent_grads)), experts)
    rows_x, gate_up_rows = unload(raw, tok_cap, pair_cap)
    steps = scatter_start(product(rows_x, gate_up_rows, True))
    rows_dy = exchange(after(sent_grads, (raw_down, steps)), experts)
    terms = scatter_end(*steps)
    hidden, sums = hidden_of(terms)
    hidden = gather_blocks(hidden)
    down_rows = unpack_one(raw_down, pair_cap)
    out_part = product(hidden, down_rows, False)
    picks = token_pairs(route, experts, tok_cap)
    out_part, rows_dy, picks = lax.optimization_barrier((out_part, rows_dy, picks))
    back_out = exchange(out_part, experts)

    back = scatter_end(*scatter_start(product(rows_dy, down_rows, True)))
    d_both = gather_blocks(backprop_of(back, sums))
    input_part = product(d_both, gate_up_rows, False)
    back_in = exchange(after(input_part, back_out), experts)

    d_both, hidden, rows_dy = after((d_both, hidden, rows_dy), input_part)
    grad_down = lax.dot_general(hidden, rows_dy, over_rows, preferred_element_type=F32)
    grad_gate = lax.dot_general(
        d_both[:, :SLOTS], rows_x, over_rows, preferred_element_type=F32
    )
    grad_up = lax.dot_general(d_both[:, SLOTS:], rows_x, over_rows, preferred_element_type=F32)
    mixed = combine(route, score, back_out, experts, tok_cap)
    input_grad = pair_rows(picks, back_in)
    return (
        mixed,
        input_grad,
        grad_gate.astype(BF16)[None],
        grad_up.astype(BF16)[None],
        grad_down.astype(BF16)[None],
    )


def solution(mesh):
    fine = Mesh(mesh.devices.reshape(4, 2, 8, 4), DP + EXPERT)
    full, rows_only = P(EXPERT, DP), P(EXPERT, None)
    grads = P(EXPERT, None, DP)
    return jax.shard_map(
        body,
        mesh=fine,
        in_specs=(full, full, rows_only, rows_only, rows_only, full, full, full),
        out_specs=(full, full, grads, grads, grads),
        check_vma=False,
    )
```
